128 devices in a mesh: lat: 8 (over x, y_hi), lon: 16 (over y_lo, z, core).
Axes of the slice: x: 4, y: 4 (y_hi: 2, y_lo: 2; y = y_hi * 2 + y_lo), z: 4, core: 2. Of those that a mesh axis runs over, the one named last changes fastest.
Arguments:
- var_tokens: bfloat16 [64, 384, 8, 1024], P('lat', 'lon'), may hold values from -6 to 6
- ocean_mask: int32 [64, 384, 2], P('lat', 'lon'), may hold values from 0 to 1, as said below
- land_mask: int32 [64, 384, 2], P('lat', 'lon'), may hold values from 0 to 1, as said below
- move_plan: int32 [8, 16, 2], P('lat', 'lon'), may hold values from -1 to 7, as said below
- agg_query: bfloat16 [1024], replicated, may hold values from -6 to 6
- agg_key: bfloat16 [1024, 1024], replicated, may hold values from -0.1875 to 0.1875
- agg_value: bfloat16 [1024, 1024], replicated, may hold values from -0.1875 to 0.1875
- agg_out: bfloat16 [1024, 1024], replicated, may hold values from -0.1875 to 0.1875
- norm_gain: bfloat16 [1024], replicated, may hold values from 0.5 to 1.5
- win_query: bfloat16 [1024, 1024], replicated, may hold values from -0.1875 to 0.1875
- win_key: bfloat16 [1024, 1024], replicated, may hold values from -0.1875 to 0.1875
- win_value: bfloat16 [1024, 1024], replicated, may hold values from -0.1875 to 0.1875
- win_out: bfloat16 [1024, 1024], replicated, may hold values from -0.1875 to 0.1875
- out_cotangent: bfloat16 [64, 384, 1024], P('lat', 'lon'), may hold values from -6 to 6
Outputs:
- layer_out: bfloat16 [64, 384, 1024], P('lat', 'lon')
- token_grad: bfloat16 [80, 384, 8, 1024], P('lat', 'lon')
The draws below stay inside these ranges and needn't reach their ends.
Inputs may be any that keep to these rules, and one draw needn't show every extreme that they name: `ocean_mask`: 0 on land patches; present ocean variables on ocean patches. `land_mask`: 0 on ocean patches; present land variables on land patches. `move_plan`: entry 0 names a row of the device's 8 patch rows handed to the next lon index (wrapping), entry 1 one handed to the previous; -1 names none; the two entries differ unless -1.
All inputs are finite; a program needn't handle non-finite values.
Results may differ from the reference program's by a relative error of at most 0.023.
Values may be sent and summed in bfloat16 or wider, within the bound.
A program may use at most 128 MiB of HBM per device.

```python
import math
import jax
import jax.numpy as jnp
from jax import lax

D = 1024
HEADS = 16
WIN = 8
VA = 4
VO = 2
VL = 2
PLAT = 8
PLON = 24
VARS = 8
NLAT = 64
NLON = 384


def land_cover(key):
    lat_key, lon_key = jax.random.split(key)
    limits = jax.random.randint(lon_key, (NLON // PLON,), 5, 90)
    limits = jnp.repeat(limits, PLON)
    rolls = jax.random.randint(lat_key, (NLAT, NLON), 0, 100)
    return (rolls < limits[None, :]).astype(jnp.int32)


def draw_ocean_mask(key, part):
    land = land_cover(key)
    key = jax.random.fold_in(key, 11)
    present = (jax.random.randint(key, (NLAT, NLON, VO), 0, 8) > 0).astype(jnp.int32)
    return ((1 - land)[:, :, None] * present).astype(jnp.int32)


def draw_land_mask(key, part):
    land = land_cover(key)
    key = jax.random.fold_in(key, 12)
    present = (jax.random.randint(key, (NLAT, NLON, VL), 0, 8) > 0).astype(jnp.int32)
    return (land[:, :, None] * present).astype(jnp.int32)


def draw_move_plan(key, part):
    key = jax.random.fold_in(key, 13)
    keys = jax.random.split(key, 4)
    shape = (NLAT // PLAT, NLON // PLON)
    east = jax.random.randint(keys[0], shape, 0, PLAT)
    west = (east + jax.random.randint(keys[1], shape, 1, PLAT)) % PLAT
    east = jnp.where(jax.random.randint(keys[2], shape, 0, 10) < 3, -1, east)
    west = jnp.where(jax.random.randint(keys[3], shape, 0, 10) < 3, -1, west)
    plan = jnp.stack([east, west], axis=-1)
    plan = plan.at[0, 0, 0].set(PLAT - 1).at[0, 0, 1].set(-1)
    return plan.astype(jnp.int32)


def levels(stream_key, extent, cuts, smallest, high):
    def one(dim, blocks):
        heights = jax.random.uniform(jax.random.fold_in(jax.random.fold_in(stream_key, 6), dim), (blocks,), jnp.float32, smallest / len(cuts), high / len(cuts))
        return jnp.repeat(jnp.exp(heights), extent[dim] // blocks).reshape((-1,) + (1,) * (len(extent) - dim - 1))

    level = one(*cuts[0])
    for cut in cuts[1:]:
        level = level * one(*cut)
    return level


def scatter_about(own_key, dims, deviation, bound, cuts=(), kind=jnp.bfloat16):
    array = jax.random.normal(own_key, dims, jnp.float32) * deviation
    if len(cuts) > 0:
        array = levels(own_key, dims, cuts, -0.22, 0.18) * array
    return jnp.clip(array, min=-bound, max=bound).astype(kind)


def setup_inputs(seed: int = 0) -> dict:
    key_of = jax.random.split(jax.random.key(seed), 15)
    var_tokens = scatter_about(key_of[0], (NLAT, NLON, VARS, D), 1.0, 6.0, ((0, 8), (1, 16)))
    ocean_mask = draw_ocean_mask(jax.random.fold_in(key_of[14], 71), 0)
    land_mask = draw_land_mask(jax.random.fold_in(key_of[14], 71), 0)
    move_plan = draw_move_plan(jax.random.fold_in(key_of[14], 71), 0)
    agg_query = scatter_about(key_of[4], (D,), 1.5, 6.0)
    agg_key = scatter_about(key_of[5], (D, D), D ** -0.5, 0.1875)
    agg_value = scatter_about(key_of[6], (D, D), D ** -0.5, 0.1875)
    agg_out = scatter_about(key_of[7], (D, D), D ** -0.5, 0.1875)
    norm_gain = jnp.clip(1.0 + 0.1 * jax.random.normal(key_of[8], (D,), jnp.float32), 0.5, 1.5).astype(jnp.bfloat16)
    win_query = scatter_about(key_of[9], (D, D), D ** -0.5, 0.1875)
    win_key = scatter_about(key_of[10], (D, D), D ** -0.5, 0.1875)
    win_value = scatter_about(key_of[11], (D, D), D ** -0.5, 0.1875)
    win_out = scatter_about(key_of[12], (D, D), D ** -0.5, 0.1875)
    out_cotangent = scatter_about(key_of[13], (NLAT, NLON, D), 1.0, 6.0, ((0, 8), (1, 16)))
    return dict(var_tokens=var_tokens, ocean_mask=ocean_mask, land_mask=land_mask, move_plan=move_plan, agg_query=agg_query, agg_key=agg_key, agg_value=agg_value, agg_out=agg_out, norm_gain=norm_gain, win_query=win_query, win_key=win_key, win_value=win_value, win_out=win_out, out_cotangent=out_cotangent)


eps = 1e-06

def aggregate(tokens, weights, agg_query, agg_key, agg_value, agg_out):
    rows, cols, count, width = tokens.shape
    head_dim = width // HEADS
    flat = tokens.reshape(rows * cols * count, width)
    keys = jnp.dot(flat, agg_key, preferred_element_type=jnp.float32).astype(jnp.bfloat16)
    values = jnp.dot(flat, agg_value, preferred_element_type=jnp.float32).astype(jnp.bfloat16)
    keys = keys.reshape(rows * cols, count, HEADS, head_dim)
    values = values.reshape(rows * cols, count, HEADS, head_dim)
    query = agg_query.reshape(HEADS, head_dim)
    scores = jnp.einsum('nvhe,he->nhv', keys.astype(jnp.float32), query.astype(jnp.float32)) / math.sqrt(head_dim)
    present = weights.reshape(rows * cols, 1, count) > 0
    scores = jnp.where(present, scores, -1e+30)
    top = lax.stop_gradient(lax.optimization_barrier(jnp.max(scores, axis=-1, keepdims=True)))
    expo = jnp.exp(scores - top)
    probs = (expo / lax.optimization_barrier(jnp.sum(expo, axis=-1, keepdims=True))).astype(jnp.bfloat16)
    mixed = jnp.einsum('nhv,nvhe->nhe', probs.astype(jnp.float32), values.astype(jnp.float32)).astype(jnp.bfloat16)
    pooled = jnp.dot(mixed.reshape(rows * cols, width), agg_out, preferred_element_type=jnp.float32)
    return pooled.astype(jnp.bfloat16).reshape(rows, cols, width)

def window_layer(cells, valid, norm_gain, win_query, win_key, win_value, win_out):
    rows, cols, width = cells.shape
    head_dim = width // HEADS
    wide = cells.astype(jnp.float32)
    scale = lax.rsqrt(lax.optimization_barrier(jnp.mean(wide * wide, axis=-1, keepdims=True)) + eps)
    normed = (wide * scale * norm_gain.astype(jnp.float32)).astype(jnp.bfloat16)
    flat = normed.reshape(rows * cols, width)

    def project(weight):
        out = jnp.dot(flat, weight, preferred_element_type=jnp.float32).astype(jnp.bfloat16)
        out = out.reshape(rows // WIN, WIN, cols // WIN, WIN, HEADS, head_dim)
        return out.transpose(0, 2, 1, 3, 4, 5).reshape(rows // WIN, cols // WIN, WIN * WIN, HEADS, head_dim)
    queries = project(win_query)
    keys = project(win_key)
    values = project(win_value)
    scores = jnp.einsum('abqhe,abkhe->abhqk', queries.astype(jnp.float32), keys.astype(jnp.float32)) / math.sqrt(head_dim)
    key_ok = jnp.repeat(valid.reshape(rows // WIN, WIN), WIN, axis=1)
    scores = jnp.where(key_ok[:, None, None, None, :], scores, -1e+30)
    top = lax.stop_gradient(lax.optimization_barrier(jnp.max(scores, axis=-1, keepdims=True)))
    expo = jnp.exp(scores - top)
    probs = (expo / lax.optimization_barrier(jnp.sum(expo, axis=-1, keepdims=True))).astype(jnp.bfloat16)
    mixed = jnp.einsum('abhqk,abkhe->abqhe', probs.astype(jnp.float32), values.astype(jnp.float32)).astype(jnp.bfloat16)
    mixed = mixed.reshape(rows // WIN, cols // WIN, WIN, WIN, width).transpose(0, 2, 1, 3, 4).reshape(rows * cols, width)
    out = wide.reshape(rows * cols, width) + jnp.dot(mixed, win_out, preferred_element_type=jnp.float32)
    return out.astype(jnp.bfloat16).reshape(rows, cols, width)

def reference(var_tokens, ocean_mask, land_mask, move_plan, agg_query, agg_key, agg_value, agg_out, norm_gain, win_query, win_key, win_value, win_out, out_cotangent):
    nlat, nlon = (var_tokens.shape[0], var_tokens.shape[1])
    weights = jnp.concatenate([jnp.ones((nlat, nlon, VA), jnp.float32), ocean_mask.astype(jnp.float32), land_mask.astype(jnp.float32)], axis=-1)

    def agg_row(pair):
        return aggregate(pair[0][None], pair[1][None], agg_query, agg_key, agg_value, agg_out)[0]
    cells = lax.map(agg_row, (var_tokens, weights))
    half = WIN // 2
    rows_all = jnp.arange(nlat + WIN, dtype=jnp.int32)
    valid = (rows_all >= half) & (rows_all < nlat + half)

    def layer(field):
        padded = jnp.pad(field, ((half, half), (0, 0), (0, 0)))
        placed = jnp.roll(padded, half, axis=1)
        out = window_layer(placed, valid, norm_gain, win_query, win_key, win_value, win_out)
        return jnp.roll(out, -half, axis=1)[half:half + nlat]
    layer_out, pull = jax.vjp(layer, cells)
    cell_grad = pull(out_cotangent)[0]

    def grad_row(triple):
        tok, weight_row, grad_cells = triple
        _, pull_row = jax.vjp(lambda t: aggregate(t, weight_row[None], agg_query, agg_key, agg_value, agg_out), tok[None])
        return pull_row(grad_cells[None])[0][0]
    token_home = lax.map(grad_row, (var_tokens, weights, cell_grad))
    n_lat = nlat // PLAT
    n_lon = nlon // PLON
    blocks = token_home.reshape(n_lat, PLAT, n_lon, PLON, VARS, D)
    east = move_plan[:, :, 0]
    west = move_plan[:, :, 1]
    row_ids = jnp.arange(PLAT, dtype=jnp.int32)
    keep = (row_ids[None, :, None] != east[:, None, :]) & (row_ids[None, :, None] != west[:, None, :])
    own = jnp.where(keep[:, :, :, None, None, None], blocks, jnp.zeros((), jnp.bfloat16))

    def sent(index):
        row = jnp.clip(index, 0, PLAT - 1).astype(jnp.int32)
        picked = jnp.take_along_axis(blocks, row[:, None, :, None, None, None], axis=1)[:, 0]
        return jnp.where((index >= 0)[:, :, None, None, None], picked, jnp.zeros((), jnp.bfloat16))
    from_west = jnp.roll(sent(east), 1, axis=1)
    from_east = jnp.roll(sent(west), -1, axis=1)
    token_grad = jnp.concatenate([own, from_west[:, None], from_east[:, None]], axis=1)
    return (layer_out, token_grad.reshape(n_lat * (PLAT + 2), nlon, VARS, D))
```

```python
import functools

import jax
import jax.numpy as jnp
from jax import lax
from jax.experimental import pallas as pl
from jax.experimental.pallas import tpu as pltpu
from jax.sharding import PartitionSpec as P

MESH = pl.DeviceIdType.MESH
HEADS = 16
WIN = 8
EPS = 1e-06
F32 = jnp.float32
BF16 = jnp.bfloat16

D = 1024
HD = D // HEADS
V = 8
PLAT = 8
PLON = 24
N = PLAT * PLON
ROW = PLON * V
LANES = 128
WIDE = 256
PACK = D + 2 * LANES
HALF = N // 2
EDGE = 16
SIDE = 80


def iota(shape, dim):
    return lax.broadcasted_iota(jnp.int32, shape, dim)


def one_hot(mask, dtype=BF16):
    return jnp.where(mask, 1.0, 0.0).astype(dtype)


def nn(a, b):
    return lax.dot_general(a, b, (((1,), (0,)), ((), ())), preferred_element_type=F32)


def nt(a, b):
    return lax.dot_general(a, b, (((1,), (1,)), ((), ())), preferred_element_type=F32)


def tn(a, b):
    return lax.dot_general(a, b, (((0,), (0,)), ((), ())), preferred_element_type=F32)


def head_rows():
    return one_hot(iota((LANES, D), 0) % HEADS == iota((LANES, D), 1) // HD)


def token_lanes(patches):
    shape = (patches, V, LANES)
    return iota(shape, 2) // HEADS == iota(shape, 1)


def over_tokens(x, op):
    for shift in (HEADS, 2 * HEADS, 4 * HEADS):
        x = op(x, pltpu.roll(x, shift, axis=1))
    return x


def fold_tokens(x, patches):
    x = x.reshape(patches, V, LANES)
    return jnp.sum(jnp.where(token_lanes(patches), x, 0.0), axis=1)


def unfold_tokens(x, patches):
    x = jnp.broadcast_to(x[:, None, :], (patches, V, LANES))
    return jnp.where(token_lanes(patches), x, 0.0).reshape(patches * V, LANES).astype(BF16)


def to_quads():
    n, m = iota((HALF, HALF), 0), iota((HALF, HALF), 1)
    return one_hot(((n % 16) // 4) * PLON + (n // 16) * 4 + n % 4 == m)


def from_quads():
    n, m = iota((HALF, HALF), 1), iota((HALF, HALF), 0)
    return one_hot(((n % 16) // 4) * PLON + (n // 16) * 4 + n % 4 == m)


def front(
    n_lat, n_lon,
    tok_hbm, ocean_ref, land_ref, plan_ref, query_ref, gain_ref,
    key_hbm, value_hbm, out_hbm, wq_hbm, wk_hbm, wv_hbm, wo_hbm, cot_hbm,
    lay_ref, pack_ref, kqt_ref,
    tok, w_key, w_value, w_out, w_q, w_k, w_v, w_o, cot,
    values, probs, mixed, heads,
    h_cot, h_cell, h_lay, h_grad, r_cot, r_cell, r_lay, r_grad,
    normed, b_q, b_k, b_v, b_mixdot, b_mix, d_q, d_k, d_v,
    move_out, move_in,
    load_sem, send_sem, recv_sem,
):
    i, j = lax.axis_index("lat"), lax.axis_index("lon")
    north, south = lax.rem(i + n_lat - 1, n_lat), lax.rem(i + 1, n_lat)
    west, east = lax.rem(j + n_lon - 1, n_lon), lax.rem(j + 1, n_lon)
    to_n, to_s, to_w, to_e = (north, j), (south, j), (i, west), (i, east)
    to_nw, to_se = (north, west), (south, east)

    def load(src, dst, slot):
        return pltpu.make_async_copy(src, dst, load_sem.at[slot])

    loads = [
        load(cot_hbm, cot, 0),
        load(key_hbm, w_key, 1),
        load(tok_hbm.at[pl.ds(HALF * V, HALF * V)], tok.at[pl.ds(HALF * V, HALF * V)], 2),
        load(value_hbm, w_value, 3),
        load(tok_hbm.at[pl.ds(0, HALF * V)], tok.at[pl.ds(0, HALF * V)], 4),
        load(out_hbm, w_out, 5),
        load(wo_hbm, w_o, 6),
        load(wq_hbm, w_q, 7),
        load(wk_hbm, w_k, 8),
        load(wv_hbm, w_v, 9),
    ]
    for k in range(6):
        loads[k].start()

    barrier = pltpu.get_barrier_semaphore()
    for to in (to_n, to_s, to_w, to_e, to_nw, to_se):
        pl.semaphore_signal(barrier, inc=1, device_id=to, device_id_type=MESH)

    heads[...] = head_rows()

    def send(src, dst, to, slot):
        return pltpu.make_async_remote_copy(
            src_ref=src, dst_ref=dst, send_sem=send_sem.at[slot], recv_sem=recv_sem.at[slot],
            device_id=to, device_id_type=MESH,
        )

    def outward(home, region, slot):
        return [
            send(home.at[pl.ds(HALF, SIDE)], region.at[pl.ds(EDGE, SIDE)], to_s, slot),
            send(home.at[pl.ds(HALF + SIDE, EDGE)], region.at[pl.ds(0, EDGE)], to_se, slot + 1),
            send(home.at[pl.ds(SIDE, EDGE)], region.at[pl.ds(HALF, EDGE)], to_e, slot + 2),
        ]

    def inward(region, home, slot):
        return [
            send(region.at[pl.ds(EDGE, SIDE)], home.at[pl.ds(HALF, SIDE)], to_n, slot),
            send(region.at[pl.ds(0, EDGE)], home.at[pl.ds(HALF + SIDE, EDGE)], to_nw, slot + 1),
            send(region.at[pl.ds(HALF, EDGE)], home.at[pl.ds(SIDE, EDGE)], to_w, slot + 2),
        ]

    send_cot = outward(h_cot, r_cot, 0)
    send_cell = outward(h_cell, r_cell, 3)
    send_lay = inward(r_lay, h_lay, 6)
    send_grad = inward(r_grad, h_grad, 9)
    send_move = [
        send(move_out.at[0], move_in.at[0], to_e, 12),
        send(move_out.at[1], move_in.at[1], to_w, 13),
    ]

    loads[0].wait()
    quads = to_quads()
    for half in (1, 0):
        rows = pl.ds(half * HALF, HALF)
        h_cot[rows, :] = nn(quads, cot[rows, :]).astype(BF16)
    r_cot[pl.ds(HALF + EDGE, SIDE), :] = h_cot[pl.ds(0, SIDE), :]
    pl.semaphore_wait(barrier, 6)
    for copy in send_cot:
        copy.start()

    loads[1].wait()
    picked = heads[...] * query_ref[...]
    key_query = nt(picked, w_key[...]) * (1.0 / HD**0.5)
    high = key_query.astype(BF16)
    kqt_ref[0:LANES, :] = high
    kqt_ref[LANES:WIDE, :] = (key_query - high.astype(F32)).astype(BF16)

    for k in range(6, 10):
        loads[k].start()

    lane_token = iota((PLON, LANES), 1) // HEADS

    def live_of(row):
        pick_o = one_hot(iota((2, LANES), 0) + 4 == iota((2, LANES), 1) // HEADS, F32)
        pick_l = one_hot(iota((2, LANES), 0) + 6 == iota((2, LANES), 1) // HEADS, F32)
        there = tn(ocean_ref[row].astype(F32), pick_o) + tn(land_ref[row].astype(F32), pick_l)
        return (lane_token < 4) | (there > 0.5)

    chunk = 2 * PLON
    fold = one_hot(iota((chunk, chunk * V), 1) // V == iota((chunk, chunk * V), 0))

    def aggregate(c):
        first = pl.multiple_of(c * chunk, 16)
        t_rows = pl.ds(pl.multiple_of(c * chunk * V, 16), chunk * V)
        tokens = tok[t_rows, :]
        both = nt(tokens, kqt_ref[...])
        scores = fold_tokens(both[:, :LANES] + both[:, LANES:], chunk)
        live = jnp.concatenate([live_of(c * 2), live_of(c * 2 + 1)], axis=0)
        scores = jnp.where(live, scores, -1e30)
        expo = jnp.exp(scores - over_tokens(scores, jnp.maximum))
        prob = expo / over_tokens(expo, jnp.add)
        probs[pl.ds(first, chunk), :] = prob
        spread = unfold_tokens(prob, chunk)
        for n in range(D // WIDE):
            cols = slice(n * WIDE, (n + 1) * WIDE)
            vals = nn(tokens, w_value[:, cols]).astype(BF16)
            values[t_rows, cols] = vals
            weighted = nn(spread, heads[:, cols]) * vals.astype(F32)
            mixed[pl.ds(first, chunk), cols] = nn(fold, weighted.astype(BF16)).astype(BF16)

    loads[3].wait()
    for half in (1, 0):
        loads[2 if half else 4].wait()

        @pl.loop(2 * half, 2 * half + 2)
        def _(c):
            aggregate(c)

        rows = pl.ds(half * HALF, HALF)
        if half:
            loads[5].wait()
        cells = nn(mixed[rows, :], w_out[...]).astype(BF16)
        h_cell[rows, :] = nn(quads, cells).astype(BF16)
        if half:
            send_cell[0].start()
            send_cell[1].start()
    send_cell[2].start()
    r_cell[pl.ds(HALF + EDGE, SIDE), :] = h_cell[pl.ds(0, SIDE), :]

    for copy in send_cot:
        copy.wait_recv()
    loads[6].wait()
    b_mixdot[...] = nt(r_cot[...], w_o[...]).astype(BF16)

    for copy in send_cell:
        copy.wait_recv()
    wide = r_cell[...].astype(F32)
    scale = lax.rsqrt(jnp.mean(wide * wide, axis=-1, keepdims=True) + EPS)
    normed[...] = (wide * scale * gain_ref[...].astype(F32)).astype(BF16)
    for slot, (weight, out) in enumerate(((w_q, b_q), (w_k, b_k), (w_v, b_v))):
        loads[7 + slot].wait()
        out[...] = nn(normed[...], weight[...]).astype(BF16)

    patches = WIN * WIN
    half_win = patches // 2
    pole = i == 0
    own_head = one_hot(iota((WIDE, WIDE), 0) // patches == iota((WIDE, WIDE), 1) // HD)
    far = (iota((patches, WIDE), 0) < half_win) != (iota((patches, WIDE), 1) % patches < half_win)
    bias = jnp.where(far & pole, -1e30, 0.0)
    lane_head = iota((patches, WIDE), 1) // HD

    def per_head(x):
        return jnp.concatenate([x] * (WIDE // HD), axis=0) * own_head

    def own_blocks(x):
        out = x[0:patches]
        for h in range(1, WIDE // HD):
            out = jnp.where(lane_head == h, x[h * patches : (h + 1) * patches], out)
        return out

    @pl.loop(0, D // WIDE)
    def _(g):
        cols = pl.ds(pl.multiple_of(g * WIDE, WIDE), WIDE)
        for w in range(N // patches):
            upper, lower = pl.ds(w * half_win, half_win), pl.ds(HALF + w * half_win, half_win)

            def get(ref):
                return jnp.concatenate([ref[upper, cols], ref[lower, cols]], axis=0)

            def put(ref, x):
                x = x.astype(BF16)
                ref[upper, cols] = x[:half_win]
                ref[lower, cols] = x[half_win:]

            keys, vals = get(b_k), get(b_v)
            queries = per_head(get(b_q))
            scores = nt(keys, queries) * (1.0 / HD**0.5) + bias
            expo = jnp.exp(scores - jnp.max(scores, axis=0, keepdims=True))
            prob = expo / jnp.sum(expo, axis=0, keepdims=True)
            prob_b = prob.astype(BF16)
            put(b_mix, own_blocks(tn(prob_b, vals)))
            mixdot = per_head(get(b_mixdot))
            d_prob = nt(vals, mixdot)
            inner = jnp.sum(d_prob * prob, axis=0, keepdims=True)
            d_score = (prob * (d_prob - inner) * (1.0 / HD**0.5)).astype(BF16)
            put(d_v, nn(prob_b, mixdot))
            put(d_k, nn(d_score, queries))
            put(d_q, own_blocks(tn(d_score, keys)))

    d_norm = nt(d_q[...], w_q[...]) + nt(d_k[...], w_k[...]) + nt(d_v[...], w_v[...])
    wide = r_cell[...].astype(F32)
    scale = lax.rsqrt(jnp.mean(wide * wide, axis=-1, keepdims=True) + EPS)
    d_unit = d_norm * gain_ref[...].astype(F32)
    along = jnp.mean(wide * d_unit, axis=-1, keepdims=True)
    grad = r_cot[...].astype(F32) + scale * d_unit - wide * (scale * scale * scale * along)
    r_grad[...] = grad.astype(BF16)
    for copy in send_grad:
        copy.start()
    h_grad[pl.ds(0, SIDE), :] = r_grad[pl.ds(HALF + EDGE, SIDE), :]

    result = r_cell[...].astype(F32) + nn(b_mix[...], w_o[...])
    r_lay[...] = result.astype(BF16)
    for copy in send_lay:
        copy.start()
    h_lay[pl.ds(0, SIDE), :] = r_lay[pl.ds(HALF + EDGE, SIDE), :]

    for copy in send_grad:
        copy.wait_recv()
    rows_of = from_quads()
    cell_grad = jnp.concatenate(
        [nn(rows_of, h_grad[0:HALF, :]), nn(rows_of, h_grad[HALF:N, :])], axis=0
    ).astype(BF16)

    def agg_back(grads, prob, values_of, patches):
        d_mixed = nt(grads, w_out[...]).astype(BF16)
        expand = one_hot(iota((patches * V, patches), 0) // V == iota((patches * V, patches), 1))
        d_prob = jnp.zeros((patches * V, LANES), F32)
        for n in range(D // WIDE):
            cols = slice(n * WIDE, (n + 1) * WIDE)
            product = nn(expand, d_mixed[:, cols]) * values_of(cols).astype(F32)
            d_prob += nt(product.astype(BF16), heads[:, cols])
        d_prob = fold_tokens(d_prob, patches)
        d_score = prob * (d_prob - over_tokens(prob * d_prob, jnp.add))
        return d_mixed, d_score

    index = (plan_ref[0, 0], plan_ref[0, 1])
    shape = (2 * PLON, N)
    wanted = jnp.where(
        iota(shape, 0) < PLON,
        jnp.where(index[0] >= 0, index[0] * PLON, -N),
        jnp.where(index[1] >= 0, index[1] * PLON - PLON, -N),
    )
    pick = one_hot(wanted + iota(shape, 0) == iota(shape, 1))
    leaving = nn(pick, cell_grad).astype(BF16)
    prob = nn(pick, probs[...].astype(BF16))

    def row_of(e, cols):
        out = values[0:ROW, cols]
        for r in range(1, PLAT):
            out = jnp.where(e == r, values[r * ROW : (r + 1) * ROW, cols], out)
        return out

    d_mixed, d_score = agg_back(
        leaving,
        prob,
        lambda cols: jnp.concatenate([row_of(e, cols) for e in index], axis=0),
        2 * PLON,
    )
    for k in range(2):
        rows = slice(k * PLON, (k + 1) * PLON)
        pad = jnp.zeros((32 - PLON, PACK), F32)
        block = jnp.concatenate([d_mixed[rows].astype(F32), prob[rows], d_score[rows]], axis=1)
        move_out[k] = jnp.concatenate([block, pad], axis=0).astype(BF16)
        send_move[k].start()

    for r in range(0, PLAT, 2):
        two = 2 * PLON
        d_mixed, d_score = (None, None)
        prob = probs[r * PLON : r * PLON + two, :]
        row = r + iota((two, 1), 0) // PLON
        kept = (row != index[0]) & (row != index[1])
        grads = jnp.where(kept, cell_grad[r * PLON : r * PLON + two].astype(F32), 0.0).astype(BF16)
        d_mixed, d_score = agg_back(
            grads, prob, lambda cols: values[r * ROW : (r + 2) * ROW, cols], two
        )
        block = jnp.concatenate([d_mixed.astype(F32), prob, d_score], axis=1)
        pad = jnp.zeros((32 - PLON, PACK), F32)
        for k in range(2):
            rows = slice(k * PLON, (k + 1) * PLON)
            pack_ref[r + k] = jnp.concatenate([block[rows], pad], axis=0).astype(BF16)

    for copy in send_lay:
        copy.wait_recv()
    for half in (0, 1):
        rows = slice(half * HALF, (half + 1) * HALF)
        lay_ref[rows, :] = nn(rows_of, h_lay[rows, :]).astype(BF16)
    for copy in send_move:
        copy.wait_recv()
    for k in range(2):
        pack_ref[PLAT + k] = move_in[k]
    for copy in send_cot + send_cell + send_lay + send_grad + send_move:
        copy.wait_send()


def back(pack_ref, value_ref, kqt_ref, lay_ref, grad_ref, lay_out_ref, heads):
    @pl.when(pl.program_id(0) == 0)
    def _():
        heads[...] = head_rows()
        lay_out_ref[...] = lay_ref[...]

    expand = one_hot(iota((ROW, 32), 0) // V == iota((ROW, 32), 1))
    for k in range(pack_ref.shape[0]):
        block = pack_ref[k]
        prob = unfold_tokens(block[:PLON, D : D + LANES].astype(F32), PLON)
        d_score = unfold_tokens(block[:PLON, D + LANES :].astype(F32), PLON)
        d_values = nn(prob, heads[...]) * nn(expand, block[:, :D])
        out = nt(d_values.astype(BF16), value_ref[...])
        out += nn(jnp.concatenate([d_score, d_score], axis=1), kqt_ref[...])
        grad_ref[k * ROW : (k + 1) * ROW, :] = out.astype(BF16)


def body(
    n_lat, n_lon,
    var_tokens, ocean_mask, land_mask, move_plan, agg_query, agg_key, agg_value, agg_out,
    norm_gain, win_query, win_key, win_value, win_out, out_cotangent,
):
    anywhere = pl.BlockSpec(memory_space=pl.ANY)
    vmem = pl.BlockSpec(memory_space=pltpu.VMEM)
    smem = pl.BlockSpec(memory_space=pltpu.SMEM)
    weight = pltpu.VMEM((D, D), BF16)
    patch = pltpu.VMEM((N, D), BF16)
    lay, pack, kqt = pl.pallas_call(
        functools.partial(front, n_lat, n_lon),
        out_shape=(
            jax.ShapeDtypeStruct((N, D), BF16),
            jax.ShapeDtypeStruct((PLAT + 2, 32, PACK), BF16),
            jax.ShapeDtypeStruct((WIDE, D), BF16),
        ),
        in_specs=[anywhere, vmem, vmem, smem, vmem, vmem] + [anywhere] * 8,
        out_specs=(vmem, vmem, vmem),
        scratch_shapes=[pltpu.VMEM((N * V, D), BF16)]
        + [weight] * 7
        + [patch, pltpu.VMEM((N * V, D), BF16), pltpu.VMEM((N, LANES), F32), patch]
        + [pltpu.VMEM((LANES, D), BF16)]
        + [patch] * 8
        + [patch] * 9
        + [pltpu.VMEM((2, 32, PACK), BF16)] * 2
        + [
            pltpu.SemaphoreType.DMA((10,)),
            pltpu.SemaphoreType.DMA((14,)),
            pltpu.SemaphoreType.DMA((14,)),
        ],
        compiler_params=pltpu.CompilerParams(
            collective_id=0, has_side_effects=True, vmem_limit_bytes=52 * 1024 * 1024
        ),
        name="front",
    )(
        var_tokens.reshape(N * V, D),
        jnp.transpose(ocean_mask, (0, 2, 1)),
        jnp.transpose(land_mask, (0, 2, 1)),
        move_plan.reshape(1, 2),
        agg_query.reshape(1, D),
        norm_gain.reshape(1, D),
        agg_key, agg_value, agg_out, win_query, win_key, win_value, win_out,
        out_cotangent.reshape(N, D),
    )

    rows = 2
    fixed = lambda shape: pl.BlockSpec(shape, lambda r: (0,) * len(shape))
    token_grad, layer_out = pl.pallas_call(
        back,
        grid=((PLAT + 2) // rows,),
        out_shape=(
            jax.ShapeDtypeStruct(((PLAT + 2) * ROW, D), BF16),
            jax.ShapeDtypeStruct((N, D), BF16),
        ),
        in_specs=[
            pl.BlockSpec((rows, 32, PACK), lambda r: (r, 0, 0)),
            fixed((D, D)),
            fixed((WIDE, D)),
            fixed((N, D)),
        ],
        out_specs=(pl.BlockSpec((rows * ROW, D), lambda r: (r, 0)), fixed((N, D))),
        scratch_shapes=[pltpu.VMEM((LANES, D), BF16)],
        compiler_params=pltpu.CompilerParams(vmem_limit_bytes=32 * 1024 * 1024),
        name="back",
    )(pack, agg_value, kqt, lay)
    return (
        layer_out.reshape(PLAT, PLON, D),
        token_grad.reshape(PLAT + 2, PLON, V, D),
    )


def solution(mesh):
    placed = P("lat", "lon", None)
    return jax.shard_map(
        functools.partial(body, mesh.shape["lat"], mesh.shape["lon"]),
        mesh=mesh,
        in_specs=(P("lat", "lon", None, None), placed, placed, placed) + (P(),) * 9 + (placed,),
        out_specs=(placed, P("lat", "lon", None, None)),
        check_vma=False,
    )
```

```python
import functools

import jax
import jax.numpy as jnp
from jax import lax
from jax.experimental import pallas as pl
from jax.experimental.pallas import tpu as pltpu
from jax.sharding import PartitionSpec as P

MESH = pl.DeviceIdType.MESH
HEADS = 16
WIN = 8
EPS = 1e-06
F32 = jnp.float32
BF16 = jnp.bfloat16

D = 1024
HD = D // HEADS
V = 8
PLAT = 8
PLON = 24
N = PLAT * PLON
ROW = PLON * V
LANES = 128
WIDE = 256
HALF = N // 2
EDGE = 16
SIDE = 80
GROUP = 32
SPAN = GROUP * V


def iota(shape, dim):
    return lax.broadcasted_iota(jnp.int32, shape, dim)


def one_hot(mask, dtype=BF16):
    return jnp.where(mask, 1.0, 0.0).astype(dtype)


def nn(a, b):
    return lax.dot_general(a, b, (((1,), (0,)), ((), ())), preferred_element_type=F32)


def nt(a, b):
    return lax.dot_general(a, b, (((1,), (1,)), ((), ())), preferred_element_type=F32)


def tn(a, b):
    return lax.dot_general(a, b, (((0,), (0,)), ((), ())), preferred_element_type=F32)


def head_rows():
    return one_hot(iota((HEADS, D), 0) == iota((HEADS, D), 1) // HD)


def stack(x):
    return jnp.concatenate([x[:, k : k + LANES] for k in range(0, x.shape[1], LANES)], axis=0)


def unstack(x):
    return jnp.concatenate([x[k : k + HEADS] for k in range(0, x.shape[0], HEADS)], axis=1)


def over_tokens(x, op):
    lane = iota(x.shape, 1)
    for step in (1, 2, 4):
        other = jnp.where(
            lane & step == 0, pltpu.roll(x, LANES - step, axis=1), pltpu.roll(x, step, axis=1)
        )
        x = op(x, other)
    return x


def to_quads():
    n, m = iota((HALF, HALF), 0), iota((HALF, HALF), 1)
    return one_hot(((n % 16) // 4) * PLON + (n // 16) * 4 + n % 4 == m)


def from_quads():
    n, m = iota((HALF, HALF), 1), iota((HALF, HALF), 0)
    return one_hot(((n % 16) // 4) * PLON + (n // 16) * 4 + n % 4 == m)


def front(
    n_lat, n_lon,
    tok_hbm, ocean_hbm, land_hbm, plan_hbm, query_hbm, gain_hbm,
    key_hbm, value_hbm, out_hbm, wq_hbm, wk_hbm, wv_hbm, wo_hbm, cot_hbm,
    lay_ref, mixdot_ref, probs_ref, scores_ref, kq_ref,
    tok, w_key, w_value, w_out, w_q, w_k, w_v, w_o, cot,
    ocean, land, query, gain, plan,
    values, probs, d_probs, mixed, d_mixed, live,
    h_cot, h_cell, h_lay, h_grad, r_cot, r_cell, r_lay, r_grad,
    normed, b_q, b_k, b_v, b_mixdot, b_mix, d_q, d_k, d_v,
    move_out, move_in, move_out_p, move_in_p,
    load_sem, send_sem, recv_sem,
):
    i, j = lax.axis_index("lat"), lax.axis_index("lon")
    north, south = lax.rem(i + n_lat - 1, n_lat), lax.rem(i + 1, n_lat)
    west, east = lax.rem(j + n_lon - 1, n_lon), lax.rem(j + 1, n_lon)
    to_n, to_s, to_w, to_e = (north, j), (south, j), (i, west), (i, east)
    to_nw, to_se = (north, west), (south, east)

    def load(src, dst, slot):
        return pltpu.make_async_copy(src, dst, load_sem.at[slot])

    upper, lower = pl.ds(0, HALF * V), pl.ds(HALF * V, HALF * V)
    loads = {
        "tok1": load(tok_hbm.at[lower], tok.at[lower], 0),
        "value": load(value_hbm, w_value, 1),
        "key": load(key_hbm, w_key, 2),
        "query": load(query_hbm, query, 3),
        "cot": load(cot_hbm, cot, 4),
        "ocean": load(ocean_hbm, ocean, 5),
        "land": load(land_hbm, land, 6),
        "tok0": load(tok_hbm.at[upper], tok.at[upper], 7),
        "out": load(out_hbm, w_out, 8),
        "wo": load(wo_hbm, w_o, 9),
        "gain": load(gain_hbm, gain, 10),
        "plan": load(plan_hbm, plan, 11),
        "wq": load(wq_hbm, w_q, 12),
        "wk": load(wk_hbm, w_k, 13),
        "wv": load(wv_hbm, w_v, 14),
    }
    early = ("tok1", "value", "key", "query", "cot", "ocean", "land")
    for name in early:
        loads[name].start()

    barrier = pltpu.get_barrier_semaphore()
    for to in (to_n, to_s, to_w, to_e, to_nw, to_se):
        pl.semaphore_signal(barrier, inc=1, device_id=to, device_id_type=MESH)

    def send(src, dst, to, slot):
        return pltpu.make_async_remote_copy(
            src_ref=src, dst_ref=dst, send_sem=send_sem.at[slot], recv_sem=recv_sem.at[slot],
            device_id=to, device_id_type=MESH,
        )

    def outward(home, region, slot):
        return [
            send(home.at[pl.ds(HALF, SIDE)], region.at[pl.ds(EDGE, SIDE)], to_s, slot),
            send(home.at[pl.ds(HALF + SIDE, EDGE)], region.at[pl.ds(0, EDGE)], to_se, slot + 1),
            send(home.at[pl.ds(SIDE, EDGE)], region.at[pl.ds(HALF, EDGE)], to_e, slot + 2),
        ]

    def inward(region, home, slot):
        return [
            send(region.at[pl.ds(EDGE, SIDE)], home.at[pl.ds(HALF, SIDE)], to_n, slot),
            send(region.at[pl.ds(0, EDGE)], home.at[pl.ds(HALF + SIDE, EDGE)], to_nw, slot + 1),
            send(region.at[pl.ds(HALF, EDGE)], home.at[pl.ds(SIDE, EDGE)], to_w, slot + 2),
        ]

    send_cot = outward(h_cot, r_cot, 0)
    send_cell = outward(h_cell, r_cell, 3)
    send_lay = inward(r_lay, h_lay, 6)
    send_grad = inward(r_grad, h_grad, 9)
    send_move = [
        send(move_out.at[0], move_in.at[0], to_e, 12),
        send(move_out.at[1], move_in.at[1], to_w, 13),
        send(move_out_p.at[0], move_in_p.at[0], to_e, 14),
        send(move_out_p.at[1], move_in_p.at[1], to_w, 15),
    ]

    loads["ocean"].wait()
    loads["land"].wait()
    rows16 = [ocean[r] for r in range(PLAT)] + [land[r] for r in range(PLAT)]
    there = jnp.concatenate(rows16, axis=0).astype(F32)
    shape = (PLON, N * V)
    there = nn(there, one_hot((iota(shape, 1) // V) % PLON == iota(shape, 0), F32))
    shape = there.shape
    line, spot = iota(shape, 0), iota(shape, 1)
    mine = ((line // 2) % PLAT == spot // ROW) & (4 + 2 * (line // 16) + line % 2 == spot % V)
    there = nn(jnp.ones((HEADS, 32), F32), jnp.where(mine, there, 0.0))
    live[...] = jnp.where(iota((HEADS, N * V), 1) % V < 4, 1.0, there)

    loads["cot"].wait()
    quads = to_quads()
    for half in (1, 0):
        rows = pl.ds(half * HALF, HALF)
        h_cot[rows, :] = nn(quads, cot[rows, :]).astype(BF16)
    r_cot[pl.ds(HALF + EDGE, SIDE), :] = h_cot[pl.ds(0, SIDE), :]
    pl.semaphore_wait(barrier, 6)
    for copy in send_cot:
        copy.start()

    loads["key"].wait()
    loads["query"].wait()
    picked = head_rows() * query[...][None, :]
    key_query = nt(picked, w_key[...]) * (1.0 / HD**0.5)
    high = key_query.astype(BF16)
    kq_ref[0:HEADS, :] = high
    kq_ref[HEADS : 2 * HEADS, :] = (key_query - high.astype(F32)).astype(BF16)

    loads["tok1"].wait()
    loads["value"].wait()
    for name in loads:
        if name not in early:
            loads[name].start()

    shape = (GROUP, SPAN)
    same_patch = iota(shape, 0) == iota(shape, 1) // V
    lane_head = iota(shape, 1) // HD
    heads_here = WIDE // HD

    for half in (1, 0):
        t_rows = slice(half * HALF * V, (half + 1) * HALF * V)
        if not half:
            loads["tok0"].wait()
        both = nt(kq_ref[...], tok[t_rows, :])
        scores = stack(both[:HEADS] + both[HEADS:])
        scores = jnp.where(stack(live[:, t_rows]) > 0.5, scores, -1e30)
        expo = jnp.exp(scores - over_tokens(scores, jnp.maximum))
        prob = unstack(expo / over_tokens(expo, jnp.add))
        probs[:, t_rows] = prob
        for n in range(D // WIDE):
            cols = slice(n * WIDE, (n + 1) * WIDE)
            vals = nn(tok[t_rows, :], w_value[:, cols]).astype(BF16)
            values[t_rows, cols] = vals
            for g in range(HALF // GROUP):
                span = slice(g * SPAN, (g + 1) * SPAN)
                weigh = [
                    jnp.where(same_patch, prob[h : h + 1, span], 0.0)
                    for h in range(n * heads_here, (n + 1) * heads_here)
                ]
                out = nn(jnp.concatenate(weigh, axis=0).astype(BF16), vals[span])
                pick = out[:GROUP]
                for h in range(1, heads_here):
                    pick = jnp.where(lane_head == h, out[h * GROUP : (h + 1) * GROUP], pick)
                first = half * HALF + g * GROUP
                mixed[first : first + GROUP, cols] = pick.astype(BF16)

        rows = pl.ds(half * HALF, HALF)
        if half:
            loads["out"].wait()
        cells = nn(mixed[rows, :], w_out[...]).astype(BF16)
        h_cell[rows, :] = nn(quads, cells).astype(BF16)
        if half:
            send_cell[0].start()
            send_cell[1].start()
    send_cell[2].start()
    r_cell[pl.ds(HALF + EDGE, SIDE), :] = h_cell[pl.ds(0, SIDE), :]

    for copy in send_cot:
        copy.wait_recv()
    loads["wo"].wait()
    b_mixdot[...] = nt(r_cot[...], w_o[...]).astype(BF16)

    for copy in send_cell:
        copy.wait_recv()
    loads["gain"].wait()
    wide = r_cell[...].astype(F32)
    scale = lax.rsqrt(jnp.mean(wide * wide, axis=-1, keepdims=True) + EPS)
    normed[...] = (wide * scale * gain[...].astype(F32)[None, :]).astype(BF16)
    for name, weight, out in (("wq", w_q, b_q), ("wk", w_k, b_k), ("wv", w_v, b_v)):
        loads[name].wait()
        out[...] = nn(normed[...], weight[...]).astype(BF16)

    patches = WIN * WIN
    half_win = patches // 2
    pole = i == 0
    own_head = one_hot(iota((WIDE, WIDE), 0) // patches == iota((WIDE, WIDE), 1) // HD)
    far = (iota((patches, WIDE), 0) < half_win) != (iota((patches, WIDE), 1) % patches < half_win)
    bias = jnp.where(far & pole, -1e30, 0.0)
    win_head = iota((patches, WIDE), 1) // HD

    def per_head(x):
        return jnp.concatenate([x] * (WIDE // HD), axis=0) * own_head

    def own_blocks(x):
        out = x[0:patches]
        for h in range(1, WIDE // HD):
            out = jnp.where(win_head == h, x[h * patches : (h + 1) * patches], out)
        return out

    @pl.loop(0, D // WIDE)
    def _(g):
        cols = pl.ds(pl.multiple_of(g * WIDE, WIDE), WIDE)
        for w in range(N // patches):
            upper, lower = pl.ds(w * half_win, half_win), pl.ds(HALF + w * half_win, half_win)

            def get(ref):
                return jnp.concatenate([ref[upper, cols], ref[lower, cols]], axis=0)

            def put(ref, x):
                x = x.astype(BF16)
                ref[upper, cols] = x[:half_win]
                ref[lower, cols] = x[half_win:]

            keys, vals = get(b_k), get(b_v)
            queries = per_head(get(b_q))
            scores = nt(keys, queries) * (1.0 / HD**0.5) + bias
            expo = jnp.exp(scores - jnp.max(scores, axis=0, keepdims=True))
            prob = expo / jnp.sum(expo, axis=0, keepdims=True)
            prob_b = prob.astype(BF16)
            put(b_mix, own_blocks(tn(prob_b, vals)))
            mixdot = per_head(get(b_mixdot))
            d_prob = nt(vals, mixdot)
            inner = jnp.sum(d_prob * prob, axis=0, keepdims=True)
            d_score = (prob * (d_prob - inner) * (1.0 / HD**0.5)).astype(BF16)
            put(d_v, nn(prob_b, mixdot))
            put(d_k, nn(d_score, queries))
            put(d_q, own_blocks(tn(d_score, keys)))

    d_norm = nt(d_q[...], w_q[...]) + nt(d_k[...], w_k[...]) + nt(d_v[...], w_v[...])
    wide = r_cell[...].astype(F32)
    scale = lax.rsqrt(jnp.mean(wide * wide, axis=-1, keepdims=True) + EPS)
    d_unit = d_norm * gain[...].astype(F32)[None, :]
    along = jnp.mean(wide * d_unit, axis=-1, keepdims=True)
    grad = r_cot[...].astype(F32) + scale * d_unit - wide * (scale * scale * scale * along)
    r_grad[...] = grad.astype(BF16)
    for copy in send_grad:
        copy.start()
    h_grad[pl.ds(0, SIDE), :] = r_grad[pl.ds(HALF + EDGE, SIDE), :]

    for copy in send_grad:
        copy.wait_recv()
    result = r_cell[...].astype(F32) + nn(b_mix[...], w_o[...])
    r_lay[...] = result.astype(BF16)
    for copy in send_lay:
        copy.start()
    h_lay[pl.ds(0, SIDE), :] = r_lay[pl.ds(HALF + EDGE, SIDE), :]
    rows_of = from_quads()
    cell_grad = jnp.concatenate(
        [nn(rows_of, h_grad[0:HALF, :]), nn(rows_of, h_grad[HALF:N, :])], axis=0
    ).astype(BF16)
    d_mixed[...] = nt(cell_grad, w_out[...]).astype(BF16)
    shape = (heads_here * GROUP, WIDE)
    own_lanes = one_hot(iota(shape, 0) // GROUP == iota(shape, 1) // HD)
    for g in range(N // GROUP):
        rows, t_rows = slice(g * GROUP, (g + 1) * GROUP), slice(g * SPAN, (g + 1) * SPAN)
        for n in range(D // WIDE):
            cols = slice(n * WIDE, (n + 1) * WIDE)
            spread = jnp.concatenate([d_mixed[rows, cols]] * heads_here, axis=0) * own_lanes
            out = nt(spread, values[t_rows, cols])
            for h in range(heads_here):
                part = jnp.where(same_patch, out[h * GROUP : (h + 1) * GROUP], 0.0)
                head = n * heads_here + h
                d_probs[head : head + 1, t_rows] = jnp.sum(part, axis=0, keepdims=True)
    prob, d_prob = stack(probs[...]), stack(d_probs[...])
    d_score = unstack(prob * (d_prob - over_tokens(prob * d_prob, jnp.add)))
    prob = probs[...]

    loads["plan"].wait()
    index = (plan[0, 0], plan[0, 1])
    shape = (PLON, N)
    for k, name in enumerate(index):
        start = jnp.where(name >= 0, name * PLON, -N)
        picked = nn(one_hot(start + iota(shape, 0) == iota(shape, 1)), d_mixed[...])
        pad = jnp.zeros((32 - PLON, D), F32)
        move_out[k] = jnp.concatenate([picked, pad], axis=0).astype(BF16)
        row = jnp.zeros((2 * HEADS, ROW), F32)
        for r in range(PLAT):
            lanes = slice(r * ROW, (r + 1) * ROW)
            here = jnp.concatenate([prob[:, lanes], d_score[:, lanes]], axis=0)
            row = jnp.where(name == r, here, row)
        pad = jnp.zeros((2 * HEADS, WIDE - ROW), F32)
        move_out_p[k] = jnp.concatenate([row, pad], axis=1).astype(BF16)
        send_move[k].start()
        send_move[2 + k].start()

    spot = iota((HEADS, N * V), 1) // ROW
    probs_ref[:, 0 : N * V] = prob.astype(BF16)
    kept = (spot != index[0]) & (spot != index[1])
    scores_ref[:, 0 : N * V] = jnp.where(kept, d_score, 0.0).astype(BF16)
    spot = iota((N, D), 0) // PLON
    kept = (spot != index[0]) & (spot != index[1])
    mixdot_ref[0:N, :] = jnp.where(kept, d_mixed[...].astype(F32), 0.0).astype(BF16)

    for copy in send_lay:
        copy.wait_recv()
    for half in (0, 1):
        rows = slice(half * HALF, (half + 1) * HALF)
        lay_ref[rows, :] = nn(rows_of, h_lay[rows, :]).astype(BF16)
    for copy in send_move:
        copy.wait_recv()
    arrived = [move_in[k].astype(F32)[:PLON] for k in range(2)]
    mixdot_ref[N : N + 2 * PLON, :] = jnp.concatenate(arrived, axis=0).astype(BF16)
    arrived = [move_in_p[k].astype(F32)[:, :ROW] for k in range(2)]
    arrived = jnp.concatenate(arrived, axis=1).astype(BF16)
    probs_ref[:, N * V :] = arrived[:HEADS]
    scores_ref[:, N * V :] = arrived[HEADS:]
    for copy in send_cot + send_cell + send_lay + send_grad + send_move:
        copy.wait_send()


def back(mixdot_ref, probs_ref, scores_ref, value_ref, kq_ref, lay_ref, grad_ref, lay_out_ref, d_values):
    @pl.when(pl.program_id(0) == 0)
    def _():
        lay_out_ref[...] = lay_ref[...]

    patches, tokens = mixdot_ref.shape[0], probs_ref.shape[1]
    expand = one_hot(iota((tokens, patches), 0) // V == iota((tokens, patches), 1))
    heads = head_rows()
    for n in range(D // WIDE):
        cols = slice(n * WIDE, (n + 1) * WIDE)
        wide = tn(probs_ref[...], heads[:, cols]) * nn(expand, mixdot_ref[:, cols])
        d_values[:, cols] = wide.astype(BF16)
    twice = jnp.concatenate([scores_ref[...]] * 2, axis=0)
    for n in range(D // WIDE):
        cols = slice(n * WIDE, (n + 1) * WIDE)
        out = nt(d_values[...], value_ref[cols, :]) + tn(twice, kq_ref[:, cols])
        grad_ref[:, cols] = out.astype(BF16)


def body(
    n_lat, n_lon,
    var_tokens, ocean_mask, land_mask, move_plan, agg_query, agg_key, agg_value, agg_out,
    norm_gain, win_query, win_key, win_value, win_out, out_cotangent,
):
    hbm = pl.BlockSpec(memory_space=pltpu.HBM)
    vmem = pl.BlockSpec(memory_space=pltpu.VMEM)
    weight = pltpu.VMEM((D, D), BF16)
    patch = pltpu.VMEM((N, D), BF16)
    tokens = (PLAT + 2) * ROW
    lay, mixdot, probs, scores, kq = pl.pallas_call(
        functools.partial(front, n_lat, n_lon),
        out_shape=(
            jax.ShapeDtypeStruct((N, D), BF16),
            jax.ShapeDtypeStruct((N + 2 * PLON, D), BF16),
            jax.ShapeDtypeStruct((HEADS, tokens), BF16),
            jax.ShapeDtypeStruct((HEADS, tokens), BF16),
            jax.ShapeDtypeStruct((2 * HEADS, D), BF16),
        ),
        in_specs=[hbm] * 14,
        out_specs=(vmem,) * 5,
        scratch_shapes=[pltpu.VMEM((N * V, D), BF16)]
        + [weight] * 7
        + [patch]
        + [pltpu.VMEM((PLAT, 2, PLON), jnp.int32)] * 2
        + [pltpu.VMEM((D,), BF16)] * 2
        + [pltpu.SMEM((1, 2), jnp.int32)]
        + [pltpu.VMEM((N * V, D), BF16)]
        + [pltpu.VMEM((HEADS, N * V), F32)] * 2
        + [patch] * 2
        + [pltpu.VMEM((HEADS, N * V), F32)]
        + [patch] * 8
        + [patch] * 9
        + [pltpu.VMEM((2, 32, D), BF16)] * 2
        + [pltpu.VMEM((2, 2 * HEADS, WIDE), BF16)] * 2
        + [
            pltpu.SemaphoreType.DMA((15,)),
            pltpu.SemaphoreType.DMA((16,)),
            pltpu.SemaphoreType.DMA((16,)),
        ],
        compiler_params=pltpu.CompilerParams(
            collective_id=0, has_side_effects=True, vmem_limit_bytes=44 * 1024 * 1024
        ),
        name="front",
    )(
        var_tokens.reshape(N * V, D),
        jnp.transpose(ocean_mask, (0, 2, 1)),
        jnp.transpose(land_mask, (0, 2, 1)),
        move_plan.reshape(1, 2),
        agg_query,
        norm_gain,
        agg_key, agg_value, agg_out, win_query, win_key, win_value, win_out,
        out_cotangent.reshape(N, D),
    )

    two = 2 * PLON
    fixed = lambda shape: pl.BlockSpec(shape, lambda r: (0,) * len(shape))
    token_grad, layer_out = pl.pallas_call(
        back,
        grid=(PLAT // 2 + 1,),
        out_shape=(
            jax.ShapeDtypeStruct((tokens, D), BF16),
            jax.ShapeDtypeStruct((N, D), BF16),
        ),
        in_specs=[
            pl.BlockSpec((two, D), lambda r: (r, 0)),
            pl.BlockSpec((HEADS, two * V), lambda r: (0, r)),
            pl.BlockSpec((HEADS, two * V), lambda r: (0, r)),
            fixed((D, D)),
            fixed((2 * HEADS, D)),
            fixed((N, D)),
        ],
        out_specs=(pl.BlockSpec((two * V, D), lambda r: (r, 0)), fixed((N, D))),
        scratch_shapes=[pltpu.VMEM((two * V, D), BF16)],
        compiler_params=pltpu.CompilerParams(vmem_limit_bytes=24 * 1024 * 1024),
        name="back",
    )(mixdot, probs, scores, agg_value, kq, lay)
    return (
        layer_out.reshape(PLAT, PLON, D),
        token_grad.reshape(PLAT + 2, PLON, V, D),
    )


def solution(mesh):
    placed = P("lat", "lon", None)
    return jax.shard_map(
        functools.partial(body, mesh.shape["lat"], mesh.shape["lon"]),
        mesh=mesh,
        in_specs=(P("lat", "lon", None, None), placed, placed, placed) + (P(),) * 9 + (placed,),
        out_specs=(placed, P("lat", "lon", None, None)),
        check_vma=False,
    )
```

```python
import functools

import jax
import jax.numpy as jnp
from jax import lax
from jax.experimental import pallas as pl
from jax.experimental.pallas import tpu as pltpu
from jax.sharding import PartitionSpec as P

MESH = pl.DeviceIdType.MESH
HEADS = 16
WIN = 8
EPS = 1e-06
F32 = jnp.float32
BF16 = jnp.bfloat16

D = 1024
HD = D // HEADS
V = 8
PLAT = 8
PLON = 24
N = PLAT * PLON
ROW = PLON * V
LANES = 128
WIDE = 256
HALF = N // 2
EDGE = 16
SIDE = 80
GROUP = 32
SPAN = GROUP * V
DEEP = D + LANES
TOKENS = (PLAT + 2) * ROW


def iota(shape, dim):
    return lax.broadcasted_iota(jnp.int32, shape, dim)


def one_hot(mask, dtype=BF16):
    return jnp.where(mask, 1.0, 0.0).astype(dtype)


def nn(a, b):
    return lax.dot_general(a, b, (((1,), (0,)), ((), ())), preferred_element_type=F32)


def nt(a, b):
    return lax.dot_general(a, b, (((1,), (1,)), ((), ())), preferred_element_type=F32)


def tn(a, b):
    return lax.dot_general(a, b, (((0,), (0,)), ((), ())), preferred_element_type=F32)


def head_rows():
    return one_hot(iota((HEADS, D), 0) == iota((HEADS, D), 1) // HD)


def stack(x):
    return jnp.concatenate([x[:, k : k + LANES] for k in range(0, x.shape[1], LANES)], axis=0)


def unstack(x):
    return jnp.concatenate([x[k : k + HEADS] for k in range(0, x.shape[0], HEADS)], axis=1)


def over_tokens(x, op):
    lane = iota(x.shape, 1)
    for step in (1, 2, 4):
        other = jnp.where(
            lane & step == 0, pltpu.roll(x, LANES - step, axis=1), pltpu.roll(x, step, axis=1)
        )
        x = op(x, other)
    return x


def to_quads():
    n, m = iota((HALF, HALF), 0), iota((HALF, HALF), 1)
    return one_hot(((n % 16) // 4) * PLON + (n // 16) * 4 + n % 4 == m)


def from_quads():
    n, m = iota((HALF, HALF), 1), iota((HALF, HALF), 0)
    return one_hot(((n % 16) // 4) * PLON + (n // 16) * 4 + n % 4 == m)


def layer(
    n_lat, n_lon,
    tok_hbm, ocean_hbm, land_hbm, plan_hbm, query_hbm, gain_hbm,
    key_hbm, value_hbm, out_hbm, wq_hbm, wk_hbm, wv_hbm, wo_hbm, cot_hbm,
    lay_ref, grad_hbm,
    tok, w_key, w_value, w_out, w_q, w_k, w_v, w_o, cot,
    ocean, land, query, gain, plan,
    values, d_values, grad_out, probs, d_probs, mixed, d_mixed, live, kq,
    h_cot, h_cell, h_lay, h_grad, r_cot, r_cell, r_lay, r_grad,
    normed, b_q, b_k, b_v, b_mixdot, b_mix, d_q, d_k, d_v,
    move_out, move_in, move_out_p, move_in_p,
    load_sem, send_sem, recv_sem,
):
    i, j = lax.axis_index("lat"), lax.axis_index("lon")
    north, south = lax.rem(i + n_lat - 1, n_lat), lax.rem(i + 1, n_lat)
    west, east = lax.rem(j + n_lon - 1, n_lon), lax.rem(j + 1, n_lon)
    to_n, to_s, to_w, to_e = (north, j), (south, j), (i, west), (i, east)
    to_nw, to_se = (north, west), (south, east)

    def load(src, dst, slot):
        return pltpu.make_async_copy(src, dst, load_sem.at[slot])

    upper, lower = pl.ds(0, HALF * V), pl.ds(HALF * V, HALF * V)
    loads = {
        "tok1": load(tok_hbm.at[lower], tok.at[lower], 0),
        "value": load(value_hbm, w_value.at[:, pl.ds(0, D)], 1),
        "key": load(key_hbm, w_key, 2),
        "query": load(query_hbm, query, 3),
        "cot": load(cot_hbm, cot, 4),
        "ocean": load(ocean_hbm, ocean, 5),
        "land": load(land_hbm, land, 6),
        "tok0": load(tok_hbm.at[upper], tok.at[upper], 7),
        "out": load(out_hbm, w_out, 8),
        "wo": load(wo_hbm, w_o, 9),
        "gain": load(gain_hbm, gain, 10),
        "plan": load(plan_hbm, plan, 11),
        "wq": load(wq_hbm, w_q, 12),
        "wk": load(wk_hbm, w_k, 13),
        "wv": load(wv_hbm, w_v, 14),
    }
    early = ("tok1", "value", "key", "query", "cot", "ocean", "land")
    for name in early:
        loads[name].start()

    barrier = pltpu.get_barrier_semaphore()
    for to in (to_n, to_s, to_w, to_e, to_nw, to_se):
        pl.semaphore_signal(barrier, inc=1, device_id=to, device_id_type=MESH)

    def send(src, dst, to, slot):
        return pltpu.make_async_remote_copy(
            src_ref=src, dst_ref=dst, send_sem=send_sem.at[slot], recv_sem=recv_sem.at[slot],
            device_id=to, device_id_type=MESH,
        )

    def outward(home, region, slot):
        return [
            send(home.at[pl.ds(HALF, SIDE)], region.at[pl.ds(EDGE, SIDE)], to_s, slot),
            send(home.at[pl.ds(HALF + SIDE, EDGE)], region.at[pl.ds(0, EDGE)], to_se, slot + 1),
            send(home.at[pl.ds(SIDE, EDGE)], region.at[pl.ds(HALF, EDGE)], to_e, slot + 2),
        ]

    def inward(region, home, slot):
        return [
            send(region.at[pl.ds(EDGE, SIDE)], home.at[pl.ds(HALF, SIDE)], to_n, slot),
            send(region.at[pl.ds(0, EDGE)], home.at[pl.ds(HALF + SIDE, EDGE)], to_nw, slot + 1),
            send(region.at[pl.ds(HALF, EDGE)], home.at[pl.ds(SIDE, EDGE)], to_w, slot + 2),
        ]

    send_cot = outward(h_cot, r_cot, 0)
    send_cell = outward(h_cell, r_cell, 3)
    send_lay = inward(r_lay, h_lay, 6)
    send_grad = inward(r_grad, h_grad, 9)
    send_move = [
        send(move_out.at[0], move_in.at[0], to_e, 12),
        send(move_out.at[1], move_in.at[1], to_w, 13),
        send(move_out_p.at[0], move_in_p.at[0], to_e, 14),
        send(move_out_p.at[1], move_in_p.at[1], to_w, 15),
    ]

    loads["ocean"].wait()
    loads["land"].wait()
    rows16 = [ocean[r] for r in range(PLAT)] + [land[r] for r in range(PLAT)]
    there = jnp.concatenate(rows16, axis=0).astype(F32)
    shape = (PLON, N * V)
    there = nn(there, one_hot((iota(shape, 1) // V) % PLON == iota(shape, 0), F32))
    shape = there.shape
    line, spot = iota(shape, 0), iota(shape, 1)
    mine = ((line // 2) % PLAT == spot // ROW) & (4 + 2 * (line // 16) + line % 2 == spot % V)
    there = nn(jnp.ones((HEADS, 32), F32), jnp.where(mine, there, 0.0))
    live[...] = jnp.where(iota((HEADS, N * V), 1) % V < 4, 1.0, there)

    loads["cot"].wait()
    quads = to_quads()
    for half in (1, 0):
        rows = pl.ds(half * HALF, HALF)
        h_cot[rows, :] = nn(quads, cot[rows, :]).astype(BF16)
    r_cot[pl.ds(HALF + EDGE, SIDE), :] = h_cot[pl.ds(0, SIDE), :]

    loads["key"].wait()
    loads["query"].wait()
    picked = head_rows() * query[...][None, :]
    key_query = nt(picked, w_key[...]) * (1.0 / HD**0.5)
    high = key_query.astype(BF16)
    low = key_query - high.astype(F32)
    both = jnp.concatenate([high.astype(F32), low, jnp.zeros((LANES - 2 * HEADS, D), F32)], axis=0)
    kq[...] = both[: 2 * HEADS].astype(BF16)
    w_value[:, D:DEEP] = both.T.astype(BF16)

    loads["tok1"].wait()
    loads["value"].wait()
    for name in loads:
        if name not in early:
            loads[name].start()
    pl.semaphore_wait(barrier, 6)
    for copy in send_cot:
        copy.start()

    shape = (GROUP, SPAN)
    same_patch = iota(shape, 0) == iota(shape, 1) // V
    lane_head = iota(shape, 1) // HD
    heads_here = WIDE // HD

    for half in (1, 0):
        t_rows = slice(half * HALF * V, (half + 1) * HALF * V)
        if not half:
            loads["tok0"].wait()
        both = nt(kq[...], tok[t_rows, :])
        scores = stack(both[:HEADS] + both[HEADS:])
        scores = jnp.where(stack(live[:, t_rows]) > 0.5, scores, -1e30)
        expo = jnp.exp(scores - over_tokens(scores, jnp.maximum))
        prob = unstack(expo / over_tokens(expo, jnp.add))
        probs[:, t_rows] = prob
        for n in range(D // WIDE):
            cols = slice(n * WIDE, (n + 1) * WIDE)
            vals = nn(tok[t_rows, :], w_value[:, cols]).astype(BF16)
            values[t_rows, cols] = vals
            for g in range(HALF // GROUP):
                span = slice(g * SPAN, (g + 1) * SPAN)
                weigh = [
                    jnp.where(same_patch, prob[h : h + 1, span], 0.0)
                    for h in range(n * heads_here, (n + 1) * heads_here)
                ]
                out = nn(jnp.concatenate(weigh, axis=0).astype(BF16), vals[span])
                pick = out[:GROUP]
                for h in range(1, heads_here):
                    pick = jnp.where(lane_head == h, out[h * GROUP : (h + 1) * GROUP], pick)
                first = half * HALF + g * GROUP
                mixed[first : first + GROUP, cols] = pick.astype(BF16)

        rows = pl.ds(half * HALF, HALF)
        if half:
            loads["out"].wait()
        cells = nn(mixed[rows, :], w_out[...]).astype(BF16)
        h_cell[rows, :] = nn(quads, cells).astype(BF16)
        if half:
            send_cell[0].start()
            send_cell[1].start()
    send_cell[2].start()
    r_cell[pl.ds(HALF + EDGE, SIDE), :] = h_cell[pl.ds(0, SIDE), :]

    for copy in send_cot:
        copy.wait_recv()
    loads["wo"].wait()
    b_mixdot[...] = nt(r_cot[...], w_o[...]).astype(BF16)

    for copy in send_cell:
        copy.wait_recv()
    loads["gain"].wait()
    wide = r_cell[...].astype(F32)
    scale = lax.rsqrt(jnp.mean(wide * wide, axis=-1, keepdims=True) + EPS)
    normed[...] = (wide * scale * gain[...].astype(F32)[None, :]).astype(BF16)
    for name, weight, out in (("wq", w_q, b_q), ("wk", w_k, b_k), ("wv", w_v, b_v)):
        loads[name].wait()
        out[...] = nn(normed[...], weight[...]).astype(BF16)

    patches = WIN * WIN
    half_win = patches // 2
    pole = i == 0
    own_head = one_hot(iota((WIDE, WIDE), 0) // patches == iota((WIDE, WIDE), 1) // HD)
    far = (iota((patches, WIDE), 0) < half_win) != (iota((patches, WIDE), 1) % patches < half_win)
    bias = jnp.where(far & pole, -1e30, 0.0)
    win_head = iota((patches, WIDE), 1) // HD

    def per_head(x):
        return jnp.concatenate([x] * (WIDE // HD), axis=0) * own_head

    def own_blocks(x):
        out = x[0:patches]
        for h in range(1, WIDE // HD):
            out = jnp.where(win_head == h, x[h * patches : (h + 1) * patches], out)
        return out

    for g in range(D // WIDE):
        cols = slice(g * WIDE, (g + 1) * WIDE)
        for w in range(N // patches):
            upper, lower = pl.ds(w * half_win, half_win), pl.ds(HALF + w * half_win, half_win)

            def get(ref):
                return jnp.concatenate([ref[upper, cols], ref[lower, cols]], axis=0)

            def put(ref, x):
                x = x.astype(BF16)
                ref[upper, cols] = x[:half_win]
                ref[lower, cols] = x[half_win:]

            keys, vals = get(b_k), get(b_v)
            queries = per_head(get(b_q))
            scores = nt(keys, queries) * (1.0 / HD**0.5) + bias
            expo = jnp.exp(scores - jnp.max(scores, axis=0, keepdims=True))
            prob = expo / jnp.sum(expo, axis=0, keepdims=True)
            prob_b = prob.astype(BF16)
            put(b_mix, own_blocks(tn(prob_b, vals)))
            mixdot = per_head(get(b_mixdot))
            d_prob = nt(vals, mixdot)
            inner = jnp.sum(d_prob * prob, axis=0, keepdims=True)
            d_score = (prob * (d_prob - inner) * (1.0 / HD**0.5)).astype(BF16)
            put(d_v, nn(prob_b, mixdot))
            put(d_k, nn(d_score, queries))
            put(d_q, own_blocks(tn(d_score, keys)))

    d_norm = nt(d_q[...], w_q[...]) + nt(d_k[...], w_k[...]) + nt(d_v[...], w_v[...])
    wide = r_cell[...].astype(F32)
    scale = lax.rsqrt(jnp.mean(wide * wide, axis=-1, keepdims=True) + EPS)
    d_unit = d_norm * gain[...].astype(F32)[None, :]
    along = jnp.mean(wide * d_unit, axis=-1, keepdims=True)
    grad = r_cot[...].astype(F32) + scale * d_unit - wide * (scale * scale * scale * along)
    r_grad[...] = grad.astype(BF16)
    for copy in send_grad:
        copy.start()
    h_grad[pl.ds(0, SIDE), :] = r_grad[pl.ds(HALF + EDGE, SIDE), :]

    result = r_cell[...].astype(F32) + nn(b_mix[...], w_o[...])
    r_lay[...] = result.astype(BF16)
    h_lay[pl.ds(0, SIDE), :] = r_lay[pl.ds(HALF + EDGE, SIDE), :]
    rows_of = from_quads()
    shape = (heads_here * GROUP, WIDE)
    own_lanes = one_hot(iota(shape, 0) // GROUP == iota(shape, 1) // HD)
    two = 2 * PLON
    expand = one_hot(iota((two * V, two), 0) // V == iota((two * V, two), 1))
    heads = head_rows()
    loads["plan"].wait()
    index = (plan[0, 0], plan[0, 1])

    def agg_back(half):
        rows, t_rows = pl.ds(half * HALF, HALF), slice(half * HALF * V, (half + 1) * HALF * V)
        cell_grad = nn(rows_of, h_grad[rows, :]).astype(BF16)
        d_mixed[rows, :] = nt(cell_grad, w_out[...]).astype(BF16)
        for g in range(half * HALF // GROUP, (half + 1) * HALF // GROUP):
            group, span = slice(g * GROUP, (g + 1) * GROUP), slice(g * SPAN, (g + 1) * SPAN)
            for n in range(D // WIDE):
                cols = slice(n * WIDE, (n + 1) * WIDE)
                spread = jnp.concatenate([d_mixed[group, cols]] * heads_here, axis=0) * own_lanes
                out = nt(spread, values[span, cols])
                for h in range(heads_here):
                    part = jnp.where(same_patch, out[h * GROUP : (h + 1) * GROUP], 0.0)
                    head = n * heads_here + h
                    d_probs[head : head + 1, span] = jnp.sum(part, axis=0, keepdims=True)
        prob, d_prob = stack(probs[:, t_rows]), stack(d_probs[:, t_rows])
        d_probs[:, t_rows] = unstack(prob * (d_prob - over_tokens(prob * d_prob, jnp.add)))

    def token_back(first, prob, d_score, here):
        t_rows = pl.ds(first * V, two * V)
        for n in range(D // WIDE):
            cols = slice(n * WIDE, (n + 1) * WIDE)
            wide = tn(prob, heads[:, cols]) * nn(expand, here[:, cols])
            d_values[t_rows, cols] = wide.astype(BF16)
        pad = jnp.zeros((LANES - 2 * HEADS, two * V), F32)
        d_values[t_rows, D:DEEP] = jnp.concatenate([d_score, d_score, pad], axis=0).T.astype(BF16)

    def multiply(first, count, slot):
        t_rows = pl.ds(first * V, count * V)
        for n in range(D // WIDE):
            cols = slice(n * WIDE, (n + 1) * WIDE)
            grad_out[t_rows, cols] = nt(d_values[t_rows, :], w_value[cols, :]).astype(BF16)
        store = pltpu.make_async_copy(grad_out.at[t_rows], grad_hbm.at[t_rows], load_sem.at[slot])
        store.start()
        return store

    def half_back(half):
        for c in range(2 * half, 2 * half + 2):
            t_rows = slice(c * two * V, (c + 1) * two * V)
            row = 2 * c + iota((two, D), 0) // PLON
            kept = (row != index[0]) & (row != index[1])
            here = d_mixed[c * two : (c + 1) * two, :].astype(F32)
            here = jnp.where(kept, here, 0.0).astype(BF16)
            row = 2 * c + iota((HEADS, two * V), 1) // ROW
            kept = (row != index[0]) & (row != index[1])
            d_score = jnp.where(kept, d_probs[:, t_rows], 0.0)
            token_back(c * two, probs[:, t_rows].astype(BF16), d_score, here)
        return multiply(half * HALF, HALF, 15 + half)

    send_grad[2].wait_recv()
    agg_back(0)
    stores = [half_back(0)]
    send_grad[0].wait_recv()
    send_grad[1].wait_recv()
    for copy in send_lay:
        copy.start()
    agg_back(1)

    shape = (PLON, N)
    for k, name in enumerate(index):
        start = jnp.where(name >= 0, name * PLON, -N)
        picked = nn(one_hot(start + iota(shape, 0) == iota(shape, 1)), d_mixed[...])
        pad = jnp.zeros((32 - PLON, D), F32)
        move_out[k] = jnp.concatenate([picked, pad], axis=0).astype(BF16)
        row = jnp.zeros((2 * HEADS, ROW), F32)
        for r in range(PLAT):
            lanes = slice(r * ROW, (r + 1) * ROW)
            here = jnp.concatenate([probs[:, lanes], d_probs[:, lanes]], axis=0)
            row = jnp.where(name == r, here, row)
        pad = jnp.zeros((2 * HEADS, WIDE - ROW), F32)
        move_out_p[k] = jnp.concatenate([row, pad], axis=1).astype(BF16)
        send_move[k].start()
        send_move[2 + k].start()

    stores.append(half_back(1))
    for copy in send_lay:
        copy.wait_recv()
    for half in (0, 1):
        rows = slice(half * HALF, (half + 1) * HALF)
        lay_ref[rows, :] = nn(rows_of, h_lay[rows, :]).astype(BF16)
    for copy in send_move:
        copy.wait_recv()
    arrived = [move_in[k].astype(F32)[:PLON] for k in range(2)]
    here = jnp.concatenate(arrived, axis=0).astype(BF16)
    arrived = [move_in_p[k].astype(F32)[:, :ROW] for k in range(2)]
    arrived = jnp.concatenate(arrived, axis=1)
    token_back(N, arrived[:HEADS].astype(BF16), arrived[HEADS:], here)
    stores.append(multiply(N, two, 17))
    for store in stores:
        store.wait()
    for copy in send_cot + send_cell + send_lay + send_grad + send_move:
        copy.wait_send()


def body(
    n_lat, n_lon,
    var_tokens, ocean_mask, land_mask, move_plan, agg_query, agg_key, agg_value, agg_out,
    norm_gain, win_query, win_key, win_value, win_out, out_cotangent,
):
    hbm = pl.BlockSpec(memory_space=pltpu.HBM)
    vmem = pl.BlockSpec(memory_space=pltpu.VMEM)
    weight = pltpu.VMEM((D, D), BF16)
    patch = pltpu.VMEM((N, D), BF16)
    layer_out, token_grad = pl.pallas_call(
        functools.partial(layer, n_lat, n_lon),
        out_shape=(
            jax.ShapeDtypeStruct((N, D), BF16),
            jax.ShapeDtypeStruct((TOKENS, D), BF16),
        ),
        in_specs=[hbm] * 14,
        out_specs=(vmem, hbm),
        scratch_shapes=[pltpu.VMEM((N * V, D), BF16)]
        + [weight, pltpu.VMEM((D, DEEP), BF16)]
        + [weight] * 5
        + [patch]
        + [pltpu.VMEM((PLAT, 2, PLON), jnp.int32)] * 2
        + [pltpu.VMEM((D,), BF16)] * 2
        + [pltpu.SMEM((1, 2), jnp.int32)]
        + [pltpu.VMEM((N * V, D), BF16), pltpu.VMEM((TOKENS, DEEP), BF16)]
        + [pltpu.VMEM((TOKENS, D), BF16)]
        + [pltpu.VMEM((HEADS, N * V), F32)] * 2
        + [patch] * 2
        + [pltpu.VMEM((HEADS, N * V), F32), pltpu.VMEM((2 * HEADS, D), BF16)]
        + [patch] * 8
        + [patch] * 9
        + [pltpu.VMEM((2, 32, D), BF16)] * 2
        + [pltpu.VMEM((2, 2 * HEADS, WIDE), BF16)] * 2
        + [
            pltpu.SemaphoreType.DMA((18,)),
            pltpu.SemaphoreType.DMA((16,)),
            pltpu.SemaphoreType.DMA((16,)),
        ],
        compiler_params=pltpu.CompilerParams(
            collective_id=0, has_side_effects=True, vmem_limit_bytes=56 * 1024 * 1024
        ),
        name="layer",
    )(
        var_tokens.reshape(N * V, D),
        jnp.transpose(ocean_mask, (0, 2, 1)),
        jnp.transpose(land_mask, (0, 2, 1)),
        move_plan.reshape(1, 2),
        agg_query,
        norm_gain,
        agg_key, agg_value, agg_out, win_query, win_key, win_value, win_out,
        out_cotangent.reshape(N, D),
    )

    return (
        layer_out.reshape(PLAT, PLON, D),
        token_grad.reshape(PLAT + 2, PLON, V, D),
    )


def solution(mesh):
    placed = P("lat", "lon", None)
    return jax.shard_map(
        functools.partial(body, mesh.shape["lat"], mesh.shape["lon"]),
        mesh=mesh,
        in_specs=(P("lat", "lon", None, None), placed, placed, placed) + (P(),) * 9 + (placed,),
        out_specs=(placed, P("lat", "lon", None, None)),
        check_vma=False,
    )
```

```python
import functools

import jax
import jax.numpy as jnp
from jax import lax
from jax.experimental import pallas as pl
from jax.experimental.pallas import tpu as pltpu
from jax.sharding import PartitionSpec as P

MESH = pl.DeviceIdType.MESH
HEADS = 16
WIN = 8
EPS = 1e-06
F32 = jnp.float32
BF16 = jnp.bfloat16

D = 1024
HD = D // HEADS
V = 8
PLAT = 8
PLON = 24
N = PLAT * PLON
ROW = PLON * V
LANES = 128
WIDE = 256
HALF = N // 2
EDGE = 16
SIDE = 80
GROUP = 32
SPAN = GROUP * V
DEEP = D + LANES
TOKENS = (PLAT + 2) * ROW


def iota(shape, dim):
    return lax.broadcasted_iota(jnp.int32, shape, dim)


def one_hot(mask, dtype=BF16):
    return jnp.where(mask, 1.0, 0.0).astype(dtype)


def nn(a, b):
    return lax.dot_general(a, b, (((1,), (0,)), ((), ())), preferred_element_type=F32)


def nt(a, b):
    return lax.dot_general(a, b, (((1,), (1,)), ((), ())), preferred_element_type=F32)


def tn(a, b):
    return lax.dot_general(a, b, (((0,), (0,)), ((), ())), preferred_element_type=F32)


def head_rows():
    return one_hot(iota((HEADS, D), 0) == iota((HEADS, D), 1) // HD)


def stack(x):
    return jnp.concatenate([x[:, k : k + LANES] for k in range(0, x.shape[1], LANES)], axis=0)


def unstack(x):
    return jnp.concatenate([x[k : k + HEADS] for k in range(0, x.shape[0], HEADS)], axis=1)


def over_tokens(x, op):
    lane = iota(x.shape, 1)
    for step in (1, 2, 4):
        other = jnp.where(
            lane & step == 0, pltpu.roll(x, LANES - step, axis=1), pltpu.roll(x, step, axis=1)
        )
        x = op(x, other)
    return x


def to_quads():
    n, m = iota((HALF, HALF), 0), iota((HALF, HALF), 1)
    return one_hot(((n % 16) // 4) * PLON + (n // 16) * 4 + n % 4 == m)


def from_quads():
    n, m = iota((HALF, HALF), 1), iota((HALF, HALF), 0)
    return one_hot(((n % 16) // 4) * PLON + (n // 16) * 4 + n % 4 == m)


def layer(
    n_lat, n_lon,
    tok_hbm, ocean_hbm, land_hbm, plan_hbm, query_hbm, gain_hbm,
    key_hbm, value_hbm, out_hbm, wq_hbm, wk_hbm, wv_hbm, wo_hbm, cot_hbm,
    lay_ref, grad_out,
    tok, w_key, w_value, w_out, w_q, w_k, w_v, w_o, cot,
    ocean, land, query, gain, plan,
    values, d_values, probs, d_probs, mixed, d_mixed, live, kq,
    h_cot, h_cell, h_lay, h_grad, r_cot, r_cell, r_lay, r_grad,
    normed, b_q, b_k, b_v, b_mixdot, b_mix, d_q, d_k, d_v,
    move_out, move_in, move_out_p, move_in_p,
    load_sem, send_sem, recv_sem,
):
    i, j = lax.axis_index("lat"), lax.axis_index("lon")
    north, south = lax.rem(i + n_lat - 1, n_lat), lax.rem(i + 1, n_lat)
    west, east = lax.rem(j + n_lon - 1, n_lon), lax.rem(j + 1, n_lon)
    to_n, to_s, to_w, to_e = (north, j), (south, j), (i, west), (i, east)
    to_nw, to_se = (north, west), (south, east)

    def load(src, dst, slot):
        return pltpu.make_async_copy(src, dst, load_sem.at[slot])

    upper, lower = pl.ds(0, HALF * V), pl.ds(HALF * V, HALF * V)
    parts = {
        "tok1": (tok_hbm.at[lower], tok.at[lower]),
        "value": (value_hbm, w_value.at[:, pl.ds(0, D)]),
        "key": (key_hbm, w_key),
        "query": (query_hbm, query),
        "ocean": (ocean_hbm, ocean),
        "land": (land_hbm, land),
        "cot": (cot_hbm, cot),
        "tok0": (tok_hbm.at[upper], tok.at[upper]),
        "out": (out_hbm, w_out),
        "wo": (wo_hbm, w_o),
        "wq": (wq_hbm, w_q),
        "wk": (wk_hbm, w_k),
        "wv": (wv_hbm, w_v),
        "gain": (gain_hbm, gain),
        "plan": (plan_hbm, plan),
    }
    loads = {name: load(*ends, k) for k, (name, ends) in enumerate(parts.items())}

    early = ("tok1", "value", "key", "query", "cot", "ocean", "land")
    for name in early:
        loads[name].start()

    barrier = pltpu.get_barrier_semaphore()
    for to in (to_n, to_s, to_w, to_e, to_nw, to_se):
        pl.semaphore_signal(barrier, inc=1, device_id=to, device_id_type=MESH)

    def send(src, dst, to, slot):
        return pltpu.make_async_remote_copy(
            src_ref=src, dst_ref=dst, send_sem=send_sem.at[slot], recv_sem=recv_sem.at[slot],
            device_id=to, device_id_type=MESH,
        )

    def outward(home, region, slot):
        return [
            send(home.at[pl.ds(HALF, SIDE)], region.at[pl.ds(EDGE, SIDE)], to_s, slot),
            send(home.at[pl.ds(HALF + SIDE, EDGE)], region.at[pl.ds(0, EDGE)], to_se, slot + 1),
            send(home.at[pl.ds(SIDE, EDGE)], region.at[pl.ds(HALF, EDGE)], to_e, slot + 2),
        ]

    def inward(region, home, slot):
        return [
            send(region.at[pl.ds(EDGE, SIDE)], home.at[pl.ds(HALF, SIDE)], to_n, slot),
            send(region.at[pl.ds(0, EDGE)], home.at[pl.ds(HALF + SIDE, EDGE)], to_nw, slot + 1),
            send(region.at[pl.ds(HALF, EDGE)], home.at[pl.ds(SIDE, EDGE)], to_w, slot + 2),
        ]

    send_cot = outward(h_cot, r_cot, 0)
    send_cell = outward(h_cell, r_cell, 3)
    send_lay = inward(r_lay, h_lay, 6)
    send_grad = inward(r_grad, h_grad, 9)
    send_move = [
        send(move_out.at[0], move_in.at[0], to_e, 12),
        send(move_out.at[1], move_in.at[1], to_w, 13),
        send(move_out_p.at[0], move_in_p.at[0], to_e, 14),
        send(move_out_p.at[1], move_in_p.at[1], to_w, 15),
    ]

    loads["tok1"].wait()
    loads["value"].wait()
    for name in loads:
        if name not in early:
            loads[name].start()

    def project_values(half):
        t_rows = slice(half * HALF * V, (half + 1) * HALF * V)
        for n in range(D // WIDE):
            cols = slice(n * WIDE, (n + 1) * WIDE)
            values[t_rows, cols] = nn(tok[t_rows, :], w_value[:, cols]).astype(BF16)

    project_values(1)

    loads["cot"].wait()
    quads = to_quads()
    for half in (1, 0):
        rows = pl.ds(half * HALF, HALF)
        h_cot[rows, :] = nn(quads, cot[rows, :]).astype(BF16)
    r_cot[pl.ds(HALF + EDGE, SIDE), :] = h_cot[pl.ds(0, SIDE), :]
    pl.semaphore_wait(barrier, 6)
    for copy in send_cot:
        copy.start()

    loads["key"].wait()
    loads["query"].wait()
    picked = head_rows() * query[...][None, :]
    key_query = nt(picked, w_key[...]) * (1.0 / HD**0.5)
    high = key_query.astype(BF16)
    low = key_query - high.astype(F32)
    kq[...] = jnp.concatenate([high.astype(F32), low], axis=0).astype(BF16)

    loads["ocean"].wait()
    loads["land"].wait()
    rows16 = [ocean[r] for r in range(PLAT)] + [land[r] for r in range(PLAT)]
    there = jnp.concatenate(rows16, axis=0).astype(F32)
    shape = (PLON, N * V)
    there = nn(there, one_hot((iota(shape, 1) // V) % PLON == iota(shape, 0), F32))
    shape = there.shape
    line, spot = iota(shape, 0), iota(shape, 1)
    mine = ((line // 2) % PLAT == spot // ROW) & (4 + 2 * (line // 16) + line % 2 == spot % V)
    there = nn(jnp.ones((HEADS, 32), F32), jnp.where(mine, there, 0.0))
    live[...] = jnp.where(iota((HEADS, N * V), 1) % V < 4, 1.0, there)

    shape = (GROUP, SPAN)
    same_patch = iota(shape, 0) == iota(shape, 1) // V
    lane_head = iota(shape, 1) // HD
    heads_here = WIDE // HD

    for half in (1, 0):
        t_rows = slice(half * HALF * V, (half + 1) * HALF * V)
        if not half:
            loads["tok0"].wait()
            project_values(0)
        both = nt(kq[...], tok[t_rows, :])
        scores = stack(both[:HEADS] + both[HEADS:])
        scores = jnp.where(stack(live[:, t_rows]) > 0.5, scores, -1e30)
        expo = jnp.exp(scores - over_tokens(scores, jnp.maximum))
        prob = unstack(expo / over_tokens(expo, jnp.add))
        probs[:, t_rows] = prob
        for n in range(D // WIDE):
            cols = slice(n * WIDE, (n + 1) * WIDE)
            vals = values[t_rows, cols]
            for g in range(HALF // GROUP):
                span = slice(g * SPAN, (g + 1) * SPAN)
                weigh = [
                    jnp.where(same_patch, prob[h : h + 1, span], 0.0)
                    for h in range(n * heads_here, (n + 1) * heads_here)
                ]
                out = nn(jnp.concatenate(weigh, axis=0).astype(BF16), vals[span])
                pick = out[:GROUP]
                for h in range(1, heads_here):
                    pick = jnp.where(lane_head == h, out[h * GROUP : (h + 1) * GROUP], pick)
                first = half * HALF + g * GROUP
                mixed[first : first + GROUP, cols] = pick.astype(BF16)

        rows = pl.ds(half * HALF, HALF)
        if half:
            loads["out"].wait()
        cells = nn(mixed[rows, :], w_out[...]).astype(BF16)
        h_cell[rows, :] = nn(quads, cells).astype(BF16)
        if half:
            send_cell[0].start()
            send_cell[1].start()
    send_cell[2].start()
    r_cell[pl.ds(HALF + EDGE, SIDE), :] = h_cell[pl.ds(0, SIDE), :]

    for copy in send_cot:
        copy.wait_recv()
    loads["wo"].wait()
    b_mixdot[...] = nt(r_cot[...], w_o[...]).astype(BF16)

    deep = jnp.concatenate([kq[...].astype(F32), jnp.zeros((LANES - 2 * HEADS, D), F32)], axis=0)
    w_value[:, D:DEEP] = deep.T.astype(BF16)

    for copy in send_cell:
        copy.wait_recv()
    loads["gain"].wait()
    wide = r_cell[...].astype(F32)
    scale = lax.rsqrt(jnp.mean(wide * wide, axis=-1, keepdims=True) + EPS)
    normed[...] = (wide * scale * gain[...].astype(F32)[None, :]).astype(BF16)
    for name, weight, out in (("wq", w_q, b_q), ("wk", w_k, b_k), ("wv", w_v, b_v)):
        loads[name].wait()
        out[...] = nn(normed[...], weight[...]).astype(BF16)

    patches = WIN * WIN
    half_win = patches // 2
    pole = i == 0
    own_head = one_hot(iota((WIDE, WIDE), 0) // patches == iota((WIDE, WIDE), 1) // HD)
    far = (iota((patches, WIDE), 0) < half_win) != (iota((patches, WIDE), 1) % patches < half_win)
    bias = jnp.where(far & pole, -1e30, 0.0)
    win_head = iota((patches, WIDE), 1) // HD

    def per_head(x):
        return jnp.concatenate([x] * (WIDE // HD), axis=0) * own_head

    def own_blocks(x):
        out = x[0:patches]
        for h in range(1, WIDE // HD):
            out = jnp.where(win_head == h, x[h * patches : (h + 1) * patches], out)
        return out

    for g in range(D // WIDE):
        cols = slice(g * WIDE, (g + 1) * WIDE)
        for w in range(N // patches):
            upper, lower = pl.ds(w * half_win, half_win), pl.ds(HALF + w * half_win, half_win)

            def get(ref):
                return jnp.concatenate([ref[upper, cols], ref[lower, cols]], axis=0)

            def put(ref, x):
                x = x.astype(BF16)
                ref[upper, cols] = x[:half_win]
                ref[lower, cols] = x[half_win:]

            keys, vals = get(b_k), get(b_v)
            queries = per_head(get(b_q))
            scores = nt(keys, queries) * (1.0 / HD**0.5) + bias
            expo = jnp.exp(scores - jnp.max(scores, axis=0, keepdims=True))
            prob = expo / jnp.sum(expo, axis=0, keepdims=True)
            prob_b = prob.astype(BF16)
            put(b_mix, own_blocks(tn(prob_b, vals)))
            mixdot = per_head(get(b_mixdot))
            d_prob = nt(vals, mixdot)
            inner = jnp.sum(d_prob * prob, axis=0, keepdims=True)
            d_score = (prob * (d_prob - inner) * (1.0 / HD**0.5)).astype(BF16)
            put(d_v, nn(prob_b, mixdot))
            put(d_k, nn(d_score, queries))
            put(d_q, own_blocks(tn(d_score, keys)))

    d_norm = nt(d_q[...], w_q[...]) + nt(d_k[...], w_k[...]) + nt(d_v[...], w_v[...])
    wide = r_cell[...].astype(F32)
    scale = lax.rsqrt(jnp.mean(wide * wide, axis=-1, keepdims=True) + EPS)
    d_unit = d_norm * gain[...].astype(F32)[None, :]
    along = jnp.mean(wide * d_unit, axis=-1, keepdims=True)
    grad = r_cot[...].astype(F32) + scale * d_unit - wide * (scale * scale * scale * along)
    r_grad[...] = grad.astype(BF16)
    for copy in send_grad:
        copy.start()
    h_grad[pl.ds(0, SIDE), :] = r_grad[pl.ds(HALF + EDGE, SIDE), :]

    result = r_cell[...].astype(F32) + nn(b_mix[...], w_o[...])
    r_lay[...] = result.astype(BF16)
    h_lay[pl.ds(0, SIDE), :] = r_lay[pl.ds(HALF + EDGE, SIDE), :]
    rows_of = from_quads()
    shape = (heads_here * GROUP, WIDE)
    own_lanes = one_hot(iota(shape, 0) // GROUP == iota(shape, 1) // HD)
    two = 2 * PLON
    expand = one_hot(iota((two * V, two), 0) // V == iota((two * V, two), 1))
    heads = head_rows()
    loads["plan"].wait()
    index = (plan[0, 0], plan[0, 1])

    def agg_back(half):
        rows, t_rows = pl.ds(half * HALF, HALF), slice(half * HALF * V, (half + 1) * HALF * V)
        cell_grad = nn(rows_of, h_grad[rows, :]).astype(BF16)
        d_mixed[rows, :] = nt(cell_grad, w_out[...]).astype(BF16)
        for g in range(half * HALF // GROUP, (half + 1) * HALF // GROUP):
            group, span = slice(g * GROUP, (g + 1) * GROUP), slice(g * SPAN, (g + 1) * SPAN)
            for n in range(D // WIDE):
                cols = slice(n * WIDE, (n + 1) * WIDE)
                spread = jnp.concatenate([d_mixed[group, cols]] * heads_here, axis=0) * own_lanes
                out = nt(spread, values[span, cols])
                for h in range(heads_here):
                    part = jnp.where(same_patch, out[h * GROUP : (h + 1) * GROUP], 0.0)
                    head = n * heads_here + h
                    d_probs[head : head + 1, span] = jnp.sum(part, axis=0, keepdims=True)
        prob, d_prob = stack(probs[:, t_rows]), stack(d_probs[:, t_rows])
        d_probs[:, t_rows] = unstack(prob * (d_prob - over_tokens(prob * d_prob, jnp.add)))

    def token_back(first, prob, d_score, here):
        t_rows = pl.ds(first * V, two * V)
        for n in range(D // WIDE):
            cols = slice(n * WIDE, (n + 1) * WIDE)
            wide = tn(prob, heads[:, cols]) * nn(expand, here[:, cols])
            d_values[t_rows, cols] = wide.astype(BF16)
        pad = jnp.zeros((LANES - 2 * HEADS, two * V), F32)
        d_values[t_rows, D:DEEP] = jnp.concatenate([d_score, d_score, pad], axis=0).T.astype(BF16)

    def multiply(first, count):
        t_rows = pl.ds(first * V, count * V)
        for n in range(D // WIDE):
            cols = slice(n * WIDE, (n + 1) * WIDE)
            grad_out[t_rows, cols] = nt(d_values[t_rows, :], w_value[cols, :]).astype(BF16)

    def half_back(half):
        for c in range(2 * half, 2 * half + 2):
            t_rows = slice(c * two * V, (c + 1) * two * V)
            row = 2 * c + iota((two, D), 0) // PLON
            kept = (row != index[0]) & (row != index[1])
            here = d_mixed[c * two : (c + 1) * two, :].astype(F32)
            here = jnp.where(kept, here, 0.0).astype(BF16)
            row = 2 * c + iota((HEADS, two * V), 1) // ROW
            kept = (row != index[0]) & (row != index[1])
            d_score = jnp.where(kept, d_probs[:, t_rows], 0.0)
            token_back(c * two, probs[:, t_rows].astype(BF16), d_score, here)
        multiply(half * HALF, HALF)

    send_grad[2].wait_recv()
    agg_back(0)
    half_back(0)
    send_grad[0].wait_recv()
    send_grad[1].wait_recv()
    for copy in send_lay:
        copy.start()
    agg_back(1)

    shape = (PLON, N)
    for k, name in enumerate(index):
        start = jnp.where(name >= 0, name * PLON, -N)
        picked = nn(one_hot(start + iota(shape, 0) == iota(shape, 1)), d_mixed[...])
        pad = jnp.zeros((32 - PLON, D), F32)
        move_out[k] = jnp.concatenate([picked, pad], axis=0).astype(BF16)
        row = jnp.zeros((2 * HEADS, ROW), F32)
        for r in range(PLAT):
            lanes = slice(r * ROW, (r + 1) * ROW)
            here = jnp.concatenate([probs[:, lanes], d_probs[:, lanes]], axis=0)
            row = jnp.where(name == r, here, row)
        pad = jnp.zeros((2 * HEADS, WIDE - ROW), F32)
        move_out_p[k] = jnp.concatenate([row, pad], axis=1).astype(BF16)
        send_move[k].start()
        send_move[2 + k].start()

    half_back(1)
    for copy in send_lay:
        copy.wait_recv()
    for half in (0, 1):
        rows = slice(half * HALF, (half + 1) * HALF)
        lay_ref[rows, :] = nn(rows_of, h_lay[rows, :]).astype(BF16)
    for copy in send_move:
        copy.wait_recv()
    arrived = [move_in[k].astype(F32)[:PLON] for k in range(2)]
    here = jnp.concatenate(arrived, axis=0).astype(BF16)
    arrived = [move_in_p[k].astype(F32)[:, :ROW] for k in range(2)]
    arrived = jnp.concatenate(arrived, axis=1)
    token_back(N, arrived[:HEADS].astype(BF16), arrived[HEADS:], here)
    multiply(N, two)
    for copy in send_cot + send_cell + send_lay + send_grad + send_move:
        copy.wait_send()


def body(
    n_lat, n_lon,
    var_tokens, ocean_mask, land_mask, move_plan, agg_query, agg_key, agg_value, agg_out,
    norm_gain, win_query, win_key, win_value, win_out, out_cotangent,
):
    hbm = pl.BlockSpec(memory_space=pltpu.HBM)
    vmem = pl.BlockSpec(memory_space=pltpu.VMEM)
    weight = pltpu.VMEM((D, D), BF16)
    patch = pltpu.VMEM((N, D), BF16)
    layer_out, token_grad = pl.pallas_call(
        functools.partial(layer, n_lat, n_lon),
        out_shape=(pltpu.VMEM((N, D), BF16), pltpu.VMEM((TOKENS, D), BF16)),
        in_specs=[hbm] * 14,
        out_specs=(vmem, vmem),
        scratch_shapes=[pltpu.VMEM((N * V, D), BF16)]
        + [weight, pltpu.VMEM((D, DEEP), BF16)]
        + [weight] * 5
        + [patch]
        + [pltpu.VMEM((PLAT, 2, PLON), jnp.int32)] * 2
        + [pltpu.VMEM((D,), BF16)] * 2
        + [pltpu.SMEM((1, 2), jnp.int32)]
        + [pltpu.VMEM((N * V, D), BF16), pltpu.VMEM((TOKENS, DEEP), BF16)]
        + [pltpu.VMEM((HEADS, N * V), F32)] * 2
        + [patch] * 2
        + [pltpu.VMEM((HEADS, N * V), F32), pltpu.VMEM((2 * HEADS, D), BF16)]
        + [patch] * 8
        + [patch] * 9
        + [pltpu.VMEM((2, 32, D), BF16)] * 2
        + [pltpu.VMEM((2, 2 * HEADS, WIDE), BF16)] * 2
        + [
            pltpu.SemaphoreType.DMA((15,)),
            pltpu.SemaphoreType.DMA((16,)),
            pltpu.SemaphoreType.DMA((16,)),
        ],
        compiler_params=pltpu.CompilerParams(
            collective_id=0, has_side_effects=True, vmem_limit_bytes=56 * 1024 * 1024
        ),
        name="layer",
    )(
        var_tokens.reshape(N * V, D),
        jnp.transpose(ocean_mask, (0, 2, 1)),
        jnp.transpose(land_mask, (0, 2, 1)),
        move_plan.reshape(1, 2),
        agg_query,
        norm_gain,
        agg_key, agg_value, agg_out, win_query, win_key, win_value, win_out,
        out_cotangent.reshape(N, D),
    )

    return (
        layer_out.reshape(PLAT, PLON, D),
        token_grad.reshape(PLAT + 2, PLON, V, D),
    )


def solution(mesh):
    placed = P("lat", "lon", None)
    return jax.shard_map(
        functools.partial(body, mesh.shape["lat"], mesh.shape["lon"]),
        mesh=mesh,
        in_specs=(P("lat", "lon", None, None), placed, placed, placed) + (P(),) * 9 + (placed,),
        out_specs=(placed, P("lat", "lon", None, None)),
        check_vma=False,
    )
```

```python
import functools

import jax
import jax.numpy as jnp
from jax import lax
from jax.experimental import pallas as pl
from jax.experimental.pallas import tpu as pltpu
from jax.sharding import PartitionSpec as P

MESH = pl.DeviceIdType.MESH
HEADS = 16
WIN = 8
EPS = 1e-06
F32 = jnp.float32
BF16 = jnp.bfloat16

D = 1024
HD = D // HEADS
V = 8
PLAT = 8
PLON = 24
N = PLAT * PLON
ROW = PLON * V
LANES = 128
WIDE = 256
HALF = N // 2
EDGE = 16
SIDE = 80
GROUP = 32
SPAN = GROUP * V
DEEP = D + LANES
TOKENS = (PLAT + 2) * ROW


def iota(shape, dim):
    return lax.broadcasted_iota(jnp.int32, shape, dim)


def one_hot(mask, dtype=BF16):
    return jnp.where(mask, 1.0, 0.0).astype(dtype)


def nn(a, b):
    return lax.dot_general(a, b, (((1,), (0,)), ((), ())), preferred_element_type=F32)


def nt(a, b):
    return lax.dot_general(a, b, (((1,), (1,)), ((), ())), preferred_element_type=F32)


def tn(a, b):
    return lax.dot_general(a, b, (((0,), (0,)), ((), ())), preferred_element_type=F32)


def head_rows():
    return one_hot(iota((HEADS, D), 0) == iota((HEADS, D), 1) // HD)


def stack(x):
    return jnp.concatenate([x[:, k : k + LANES] for k in range(0, x.shape[1], LANES)], axis=0)


def unstack(x):
    return jnp.concatenate([x[k : k + HEADS] for k in range(0, x.shape[0], HEADS)], axis=1)


def over_tokens(x, op):
    lane = iota(x.shape, 1)
    for step in (1, 2, 4):
        other = jnp.where(
            lane & step == 0, pltpu.roll(x, LANES - step, axis=1), pltpu.roll(x, step, axis=1)
        )
        x = op(x, other)
    return x


def to_quads():
    n, m = iota((HALF, HALF), 0), iota((HALF, HALF), 1)
    return one_hot(((n % 16) // 4) * PLON + (n // 16) * 4 + n % 4 == m)


def from_quads():
    n, m = iota((HALF, HALF), 1), iota((HALF, HALF), 0)
    return one_hot(((n % 16) // 4) * PLON + (n // 16) * 4 + n % 4 == m)


def layer(
    n_lat, n_lon,
    tok_hbm, ocean_hbm, land_hbm, plan_hbm, query_hbm, gain_hbm,
    key_hbm, value_hbm, out_hbm, wq_hbm, wk_hbm, wv_hbm, wo_hbm, cot_hbm,
    lay_ref, grad_out,
    tok, w_key, w_value, w_out, w_q, w_k, w_v, w_o, cot,
    ocean, land, query, gain, plan,
    values, d_values, probs, d_probs, mixed, d_mixed, live, kq,
    h_cot, h_cell, h_lay, h_grad, r_cot, r_cell, r_lay, r_grad,
    normed, b_q, b_k, b_v, b_mixdot, b_mix, d_q, d_k, d_v,
    move_out, move_in, move_out_p, move_in_p,
    load_sem, send_sem, recv_sem,
):
    i, j = lax.axis_index("lat"), lax.axis_index("lon")
    north, south = lax.rem(i + n_lat - 1, n_lat), lax.rem(i + 1, n_lat)
    west, east = lax.rem(j + n_lon - 1, n_lon), lax.rem(j + 1, n_lon)
    to_n, to_s, to_w, to_e = (north, j), (south, j), (i, west), (i, east)
    to_nw, to_se = (north, west), (south, east)

    def load(src, dst, slot):
        return pltpu.make_async_copy(src, dst, load_sem.at[slot])

    upper, lower = pl.ds(0, HALF * V), pl.ds(HALF * V, HALF * V)
    parts = {
        "tok1": (tok_hbm.at[lower], tok.at[lower]),
        "value": (value_hbm, w_value.at[:, pl.ds(0, D)]),
        "key": (key_hbm, w_key),
        "query": (query_hbm, query),
        "ocean": (ocean_hbm, ocean),
        "land": (land_hbm, land),
        "cot": (cot_hbm, cot),
        "tok0": (tok_hbm.at[upper], tok.at[upper]),
        "out": (out_hbm, w_out),
        "wo": (wo_hbm, w_o),
        "wq": (wq_hbm, w_q),
        "wk": (wk_hbm, w_k),
        "wv": (wv_hbm, w_v),
        "gain": (gain_hbm, gain),
        "plan": (plan_hbm, plan),
    }
    loads = {name: load(*ends, k) for k, (name, ends) in enumerate(parts.items())}

    early = ("cot", "tok1", "value", "key", "query", "ocean", "land")
    for name in early:
        loads[name].start()

    barrier = pltpu.get_barrier_semaphore()
    for to in (to_n, to_s, to_w, to_e, to_nw, to_se):
        pl.semaphore_signal(barrier, inc=1, device_id=to, device_id_type=MESH)

    def send(src, dst, to, slot):
        return pltpu.make_async_remote_copy(
            src_ref=src, dst_ref=dst, send_sem=send_sem.at[slot], recv_sem=recv_sem.at[slot],
            device_id=to, device_id_type=MESH,
        )

    def outward(home, region, slot):
        return [
            send(home.at[pl.ds(HALF, SIDE)], region.at[pl.ds(EDGE, SIDE)], to_s, slot),
            send(home.at[pl.ds(HALF + SIDE, EDGE)], region.at[pl.ds(0, EDGE)], to_se, slot + 1),
            send(home.at[pl.ds(SIDE, EDGE)], region.at[pl.ds(HALF, EDGE)], to_e, slot + 2),
        ]

    def inward(region, home, slot):
        return [
            send(region.at[pl.ds(EDGE, SIDE)], home.at[pl.ds(HALF, SIDE)], to_n, slot),
            send(region.at[pl.ds(0, EDGE)], home.at[pl.ds(HALF + SIDE, EDGE)], to_nw, slot + 1),
            send(region.at[pl.ds(HALF, EDGE)], home.at[pl.ds(SIDE, EDGE)], to_w, slot + 2),
        ]

    send_cot = outward(h_cot, r_cot, 0)
    send_cell = outward(h_cell, r_cell, 3)
    send_lay = inward(r_lay, h_lay, 6)
    send_grad = inward(r_grad, h_grad, 9)
    send_move = [
        send(move_out.at[0], move_in.at[0], to_e, 12),
        send(move_out.at[1], move_in.at[1], to_w, 13),
        send(move_out_p.at[0], move_in_p.at[0], to_e, 14),
        send(move_out_p.at[1], move_in_p.at[1], to_w, 15),
    ]

    loads["cot"].wait()
    quads = to_quads()
    for half in (1, 0):
        rows = pl.ds(half * HALF, HALF)
        h_cot[rows, :] = nn(quads, cot[rows, :]).astype(BF16)
    r_cot[pl.ds(HALF + EDGE, SIDE), :] = h_cot[pl.ds(0, SIDE), :]

    loads["tok1"].wait()
    loads["value"].wait()
    for name in loads:
        if name not in early:
            loads[name].start()

    def project_values(half, blocks=range(D // WIDE)):
        t_rows = slice(half * HALF * V, (half + 1) * HALF * V)
        for n in blocks:
            cols = slice(n * WIDE, (n + 1) * WIDE)
            values[t_rows, cols] = nn(tok[t_rows, :], w_value[:, cols]).astype(BF16)

    project_values(1, range(1))
    pl.semaphore_wait(barrier, 6)
    for copy in send_cot:
        copy.start()
    project_values(1, range(1, D // WIDE))

    loads["key"].wait()
    loads["query"].wait()
    picked = head_rows() * query[...][None, :]
    key_query = nt(picked, w_key[...]) * (1.0 / HD**0.5)
    high = key_query.astype(BF16)
    low = key_query - high.astype(F32)
    kq[...] = jnp.concatenate([high.astype(F32), low], axis=0).astype(BF16)

    loads["ocean"].wait()
    loads["land"].wait()
    rows16 = [ocean[r] for r in range(PLAT)] + [land[r] for r in range(PLAT)]
    there = jnp.concatenate(rows16, axis=0).astype(F32)
    shape = (PLON, N * V)
    there = nn(there, one_hot((iota(shape, 1) // V) % PLON == iota(shape, 0), F32))
    shape = there.shape
    line, spot = iota(shape, 0), iota(shape, 1)
    mine = ((line // 2) % PLAT == spot // ROW) & (4 + 2 * (line // 16) + line % 2 == spot % V)
    there = nn(jnp.ones((HEADS, 32), F32), jnp.where(mine, there, 0.0))
    live[...] = jnp.where(iota((HEADS, N * V), 1) % V < 4, 1.0, there)

    shape = (GROUP, SPAN)
    same_patch = iota(shape, 0) == iota(shape, 1) // V
    lane_head = iota(shape, 1) // HD
    heads_here = WIDE // HD

    for half in (1, 0):
        t_rows = slice(half * HALF * V, (half + 1) * HALF * V)
        if not half:
            loads["tok0"].wait()
            project_values(0)
        both = nt(kq[...], tok[t_rows, :])
        scores = stack(both[:HEADS] + both[HEADS:])
        scores = jnp.where(stack(live[:, t_rows]) > 0.5, scores, -1e30)
        expo = jnp.exp(scores - over_tokens(scores, jnp.maximum))
        prob = unstack(expo / over_tokens(expo, jnp.add))
        probs[:, t_rows] = prob
        for n in range(D // WIDE):
            cols = slice(n * WIDE, (n + 1) * WIDE)
            vals = values[t_rows, cols]
            for g in range(HALF // GROUP):
                span = slice(g * SPAN, (g + 1) * SPAN)
                weigh = [
                    jnp.where(same_patch, prob[h : h + 1, span], 0.0)
                    for h in range(n * heads_here, (n + 1) * heads_here)
                ]
                out = nn(jnp.concatenate(weigh, axis=0).astype(BF16), vals[span])
                pick = out[:GROUP]
                for h in range(1, heads_here):
                    pick = jnp.where(lane_head == h, out[h * GROUP : (h + 1) * GROUP], pick)
                first = half * HALF + g * GROUP
                mixed[first : first + GROUP, cols] = pick.astype(BF16)

        rows = pl.ds(half * HALF, HALF)
        if half:
            loads["out"].wait()
        cells = nn(mixed[rows, :], w_out[...]).astype(BF16)
        h_cell[rows, :] = nn(quads, cells).astype(BF16)
        if half:
            send_cell[0].start()
            send_cell[1].start()
    send_cell[2].start()
    r_cell[pl.ds(HALF + EDGE, SIDE), :] = h_cell[pl.ds(0, SIDE), :]

    for copy in send_cot:
        copy.wait_recv()
    loads["wo"].wait()
    b_mixdot[...] = nt(r_cot[...], w_o[...]).astype(BF16)

    deep = jnp.concatenate([kq[...].astype(F32), jnp.zeros((LANES - 2 * HEADS, D), F32)], axis=0)
    w_value[:, D:DEEP] = deep.T.astype(BF16)

    for copy in send_cell:
        copy.wait_recv()
    loads["gain"].wait()
    wide = r_cell[...].astype(F32)
    scale = lax.rsqrt(jnp.mean(wide * wide, axis=-1, keepdims=True) + EPS)
    normed[...] = (wide * scale * gain[...].astype(F32)[None, :]).astype(BF16)
    for name, weight, out in (("wq", w_q, b_q), ("wk", w_k, b_k), ("wv", w_v, b_v)):
        loads[name].wait()
        out[...] = nn(normed[...], weight[...]).astype(BF16)

    patches = WIN * WIN
    half_win = patches // 2
    pole = i == 0
    own_head = one_hot(iota((WIDE, WIDE), 0) // patches == iota((WIDE, WIDE), 1) // HD)
    far = (iota((patches, WIDE), 0) < half_win) != (iota((patches, WIDE), 1) % patches < half_win)
    bias = jnp.where(far & pole, -1e30, 0.0)
    win_head = iota((patches, WIDE), 1) // HD

    def per_head(x):
        return jnp.concatenate([x] * (WIDE // HD), axis=0) * own_head

    def own_blocks(x):
        out = x[0:patches]
        for h in range(1, WIDE // HD):
            out = jnp.where(win_head == h, x[h * patches : (h + 1) * patches], out)
        return out

    wins = range(N // patches)
    for g in range(D // WIDE):
        cols = slice(g * WIDE, (g + 1) * WIDE)

        def get(ref, w):
            upper = ref[w * half_win : (w + 1) * half_win, cols]
            lower = ref[HALF + w * half_win : HALF + (w + 1) * half_win, cols]
            return jnp.concatenate([upper, lower], axis=0)

        def put(ref, w, x):
            x = x.astype(BF16)
            ref[w * half_win : (w + 1) * half_win, cols] = x[:half_win]
            ref[HALF + w * half_win : HALF + (w + 1) * half_win, cols] = x[half_win:]

        keys, vals = [get(b_k, w) for w in wins], [get(b_v, w) for w in wins]
        queries = [per_head(get(b_q, w)) for w in wins]
        scores = [nt(keys[w], queries[w]) * (1.0 / HD**0.5) + bias for w in wins]
        mixdot = [per_head(get(b_mixdot, w)) for w in wins]
        d_prob = [nt(vals[w], mixdot[w]) for w in wins]
        expo = [jnp.exp(scores[w] - jnp.max(scores[w], axis=0, keepdims=True)) for w in wins]
        prob = [expo[w] / jnp.sum(expo[w], axis=0, keepdims=True) for w in wins]
        prob_b = [prob[w].astype(BF16) for w in wins]
        for w in wins:
            put(d_v, w, nn(prob_b[w], mixdot[w]))
        inner = [jnp.sum(d_prob[w] * prob[w], axis=0, keepdims=True) for w in wins]
        d_score = [
            (prob[w] * (d_prob[w] - inner[w]) * (1.0 / HD**0.5)).astype(BF16) for w in wins
        ]
        for w in wins:
            put(b_mix, w, own_blocks(tn(prob_b[w], vals[w])))
        for w in wins:
            put(d_k, w, nn(d_score[w], queries[w]))
        for w in wins:
            put(d_q, w, own_blocks(tn(d_score[w], keys[w])))

    d_norm = nt(d_q[...], w_q[...]) + nt(d_k[...], w_k[...]) + nt(d_v[...], w_v[...])
    wide = r_cell[...].astype(F32)
    scale = lax.rsqrt(jnp.mean(wide * wide, axis=-1, keepdims=True) + EPS)
    d_unit = d_norm * gain[...].astype(F32)[None, :]
    along = jnp.mean(wide * d_unit, axis=-1, keepdims=True)
    grad = r_cot[...].astype(F32) + scale * d_unit - wide * (scale * scale * scale * along)
    r_grad[...] = grad.astype(BF16)
    for copy in send_grad:
        copy.start()
    h_grad[pl.ds(0, SIDE), :] = r_grad[pl.ds(HALF + EDGE, SIDE), :]

    result = r_cell[...].astype(F32) + nn(b_mix[...], w_o[...])
    r_lay[...] = result.astype(BF16)
    h_lay[pl.ds(0, SIDE), :] = r_lay[pl.ds(HALF + EDGE, SIDE), :]
    rows_of = from_quads()
    shape = (heads_here * GROUP, WIDE)
    own_lanes = one_hot(iota(shape, 0) // GROUP == iota(shape, 1) // HD)
    two = 2 * PLON
    expand = one_hot(iota((two * V, two), 0) // V == iota((two * V, two), 1))
    heads = head_rows()
    loads["plan"].wait()
    index = (plan[0, 0], plan[0, 1])

    def agg_back(half):
        rows, t_rows = pl.ds(half * HALF, HALF), slice(half * HALF * V, (half + 1) * HALF * V)
        cell_grad = nn(rows_of, h_grad[rows, :]).astype(BF16)
        d_mixed[rows, :] = nt(cell_grad, w_out[...]).astype(BF16)
        for g in range(half * HALF // GROUP, (half + 1) * HALF // GROUP):
            group, span = slice(g * GROUP, (g + 1) * GROUP), slice(g * SPAN, (g + 1) * SPAN)
            for n in range(D // WIDE):
                cols = slice(n * WIDE, (n + 1) * WIDE)
                spread = jnp.concatenate([d_mixed[group, cols]] * heads_here, axis=0) * own_lanes
                out = nt(spread, values[span, cols])
                for h in range(heads_here):
                    part = jnp.where(same_patch, out[h * GROUP : (h + 1) * GROUP], 0.0)
                    head = n * heads_here + h
                    d_probs[head : head + 1, span] = jnp.sum(part, axis=0, keepdims=True)
        prob, d_prob = stack(probs[:, t_rows]), stack(d_probs[:, t_rows])
        d_probs[:, t_rows] = unstack(prob * (d_prob - over_tokens(prob * d_prob, jnp.add)))

    def token_back(first, prob, d_score, here):
        t_rows = pl.ds(first * V, two * V)
        for n in range(D // WIDE):
            cols = slice(n * WIDE, (n + 1) * WIDE)
            wide = tn(prob, heads[:, cols]) * nn(expand, here[:, cols])
            d_values[t_rows, cols] = wide.astype(BF16)
        pad = jnp.zeros((LANES - 2 * HEADS, two * V), F32)
        d_values[t_rows, D:DEEP] = jnp.concatenate([d_score, d_score, pad], axis=0).T.astype(BF16)

    def multiply(first, count):
        t_rows = pl.ds(first * V, count * V)
        for n in range(D // WIDE):
            cols = slice(n * WIDE, (n + 1) * WIDE)
            grad_out[t_rows, cols] = nt(d_values[t_rows, :], w_value[cols, :]).astype(BF16)

    def half_back(half):
        for c in range(2 * half, 2 * half + 2):
            t_rows = slice(c * two * V, (c + 1) * two * V)
            row = 2 * c + iota((two, D), 0) // PLON
            kept = (row != index[0]) & (row != index[1])
            here = d_mixed[c * two : (c + 1) * two, :].astype(F32)
            here = jnp.where(kept, here, 0.0).astype(BF16)
            row = 2 * c + iota((HEADS, two * V), 1) // ROW
            kept = (row != index[0]) & (row != index[1])
            d_score = jnp.where(kept, d_probs[:, t_rows], 0.0)
            token_back(c * two, probs[:, t_rows].astype(BF16), d_score, here)
        multiply(half * HALF, HALF)

    send_grad[2].wait_recv()
    agg_back(0)
    half_back(0)
    for copy in send_lay:
        copy.start()
    send_grad[0].wait_recv()
    send_grad[1].wait_recv()
    agg_back(1)

    shape = (PLON, N)
    for k, name in enumerate(index):
        start = jnp.where(name >= 0, name * PLON, -N)
        picked = nn(one_hot(start + iota(shape, 0) == iota(shape, 1)), d_mixed[...])
        pad = jnp.zeros((32 - PLON, D), F32)
        move_out[k] = jnp.concatenate([picked, pad], axis=0).astype(BF16)
        row = jnp.zeros((2 * HEADS, ROW), F32)
        for r in range(PLAT):
            lanes = slice(r * ROW, (r + 1) * ROW)
            here = jnp.concatenate([probs[:, lanes], d_probs[:, lanes]], axis=0)
            row = jnp.where(name == r, here, row)
        pad = jnp.zeros((2 * HEADS, WIDE - ROW), F32)
        move_out_p[k] = jnp.concatenate([row, pad], axis=1).astype(BF16)
        send_move[k].start()
        send_move[2 + k].start()

    half_back(1)
    for copy in send_move:
        copy.wait_recv()
    arrived = [move_in[k].astype(F32)[:PLON] for k in range(2)]
    here = jnp.concatenate(arrived, axis=0).astype(BF16)
    arrived = [move_in_p[k].astype(F32)[:, :ROW] for k in range(2)]
    arrived = jnp.concatenate(arrived, axis=1)
    token_back(N, arrived[:HEADS].astype(BF16), arrived[HEADS:], here)
    multiply(N, two)
    for copy in send_lay:
        copy.wait_recv()
    for half in (0, 1):
        rows = slice(half * HALF, (half + 1) * HALF)
        lay_ref[rows, :] = nn(rows_of, h_lay[rows, :]).astype(BF16)
    for copy in send_cot + send_cell + send_lay + send_grad + send_move:
        copy.wait_send()


def body(
    n_lat, n_lon,
    var_tokens, ocean_mask, land_mask, move_plan, agg_query, agg_key, agg_value, agg_out,
    norm_gain, win_query, win_key, win_value, win_out, out_cotangent,
):
    hbm = pl.BlockSpec(memory_space=pltpu.HBM)
    vmem = pl.BlockSpec(memory_space=pltpu.VMEM)
    weight = pltpu.VMEM((D, D), BF16)
    patch = pltpu.VMEM((N, D), BF16)
    layer_out, token_grad = pl.pallas_call(
        functools.partial(layer, n_lat, n_lon),
        out_shape=(pltpu.VMEM((N, D), BF16), pltpu.VMEM((TOKENS, D), BF16)),
        in_specs=[hbm] * 14,
        out_specs=(vmem, vmem),
        scratch_shapes=[pltpu.VMEM((N * V, D), BF16)]
        + [weight, pltpu.VMEM((D, DEEP), BF16)]
        + [weight] * 5
        + [patch]
        + [pltpu.VMEM((PLAT, 2, PLON), jnp.int32)] * 2
        + [pltpu.VMEM((D,), BF16)] * 2
        + [pltpu.SMEM((1, 2), jnp.int32)]
        + [pltpu.VMEM((N * V, D), BF16), pltpu.VMEM((TOKENS, DEEP), BF16)]
        + [pltpu.VMEM((HEADS, N * V), F32)] * 2
        + [patch] * 2
        + [pltpu.VMEM((HEADS, N * V), F32), pltpu.VMEM((2 * HEADS, D), BF16)]
        + [patch] * 8
        + [patch] * 9
        + [pltpu.VMEM((2, 32, D), BF16)] * 2
        + [pltpu.VMEM((2, 2 * HEADS, WIDE), BF16)] * 2
        + [
            pltpu.SemaphoreType.DMA((15,)),
            pltpu.SemaphoreType.DMA((16,)),
            pltpu.SemaphoreType.DMA((16,)),
        ],
        compiler_params=pltpu.CompilerParams(
            collective_id=0, has_side_effects=True, vmem_limit_bytes=56 * 1024 * 1024
        ),
        name="layer",
    )(
        var_tokens.reshape(N * V, D),
        jnp.transpose(ocean_mask, (0, 2, 1)),
        jnp.transpose(land_mask, (0, 2, 1)),
        move_plan.reshape(1, 2),
        agg_query,
        norm_gain,
        agg_key, agg_value, agg_out, win_query, win_key, win_value, win_out,
        out_cotangent.reshape(N, D),
    )

    return (
        layer_out.reshape(PLAT, PLON, D),
        token_grad.reshape(PLAT + 2, PLON, V, D),
    )


def solution(mesh):
    placed = P("lat", "lon", None)
    return jax.shard_map(
        functools.partial(body, mesh.shape["lat"], mesh.shape["lon"]),
        mesh=mesh,
        in_specs=(P("lat", "lon", None, None), placed, placed, placed) + (P(),) * 9 + (placed,),
        out_specs=(placed, P("lat", "lon", None, None)),
        check_vma=False,
    )
```

```python
import functools

import jax
import jax.numpy as jnp
from jax import lax
from jax.experimental import pallas as pl
from jax.experimental.pallas import tpu as pltpu
from jax.sharding import PartitionSpec as P

MESH = pl.DeviceIdType.MESH
HEADS = 16
WIN = 8
EPS = 1e-06
F32 = jnp.float32
BF16 = jnp.bfloat16

D = 1024
HD = D // HEADS
V = 8
PLAT = 8
PLON = 24
N = PLAT * PLON
ROW = PLON * V
LANES = 128
WIDE = 256
HALF = N // 2
EDGE = 16
SIDE = 80
GROUP = 32
SPAN = GROUP * V
DEEP = D + LANES
TOKENS = (PLAT + 2) * ROW


def iota(shape, dim):
    return lax.broadcasted_iota(jnp.int32, shape, dim)


def one_hot(mask, dtype=BF16):
    return jnp.where(mask, 1.0, 0.0).astype(dtype)


def nn(a, b):
    return lax.dot_general(a, b, (((1,), (0,)), ((), ())), preferred_element_type=F32)


def nt(a, b):
    return lax.dot_general(a, b, (((1,), (1,)), ((), ())), preferred_element_type=F32)


def tn(a, b):
    return lax.dot_general(a, b, (((0,), (0,)), ((), ())), preferred_element_type=F32)


def head_rows():
    return one_hot(iota((HEADS, D), 0) == iota((HEADS, D), 1) // HD)


def stack(x):
    return jnp.concatenate([x[:, k : k + LANES] for k in range(0, x.shape[1], LANES)], axis=0)


def unstack(x):
    return jnp.concatenate([x[k : k + HEADS] for k in range(0, x.shape[0], HEADS)], axis=1)


def over_tokens(x, op):
    lane = iota(x.shape, 1)
    for step in (1, 2, 4):
        other = jnp.where(
            lane & step == 0, pltpu.roll(x, LANES - step, axis=1), pltpu.roll(x, step, axis=1)
        )
        x = op(x, other)
    return x


def to_quads():
    n, m = iota((HALF, HALF), 0), iota((HALF, HALF), 1)
    return one_hot(((n % 16) // 4) * PLON + (n // 16) * 4 + n % 4 == m)


def from_quads():
    n, m = iota((HALF, HALF), 1), iota((HALF, HALF), 0)
    return one_hot(((n % 16) // 4) * PLON + (n // 16) * 4 + n % 4 == m)


def layer(
    n_lat, n_lon,
    tok_hbm, ocean_hbm, land_hbm, plan_hbm, query_hbm, gain_hbm,
    key_hbm, value_hbm, out_hbm, wq_hbm, wk_hbm, wv_hbm, wo_hbm, cot_hbm,
    lay_ref, grad_out,
    tok, w_key, w_value, w_out, w_q, w_k, w_v, w_o, cot,
    ocean, land, query, gain, plan,
    values, d_values, probs, d_probs, mixed, d_mixed, live, kq,
    h_cot, h_cell, h_lay, h_grad, r_cot, r_cell, r_lay, r_grad,
    normed, b_q, b_k, b_v, b_mixdot, b_mix, d_q, d_k, d_v,
    move_out, move_in, move_out_p, move_in_p,
    load_sem, send_sem, recv_sem,
):
    i, j = lax.axis_index("lat"), lax.axis_index("lon")
    north, south = lax.rem(i + n_lat - 1, n_lat), lax.rem(i + 1, n_lat)
    west, east = lax.rem(j + n_lon - 1, n_lon), lax.rem(j + 1, n_lon)
    to_n, to_s, to_w, to_e = (north, j), (south, j), (i, west), (i, east)
    to_nw, to_se = (north, west), (south, east)

    def load(src, dst, slot):
        return pltpu.make_async_copy(src, dst, load_sem.at[slot])

    upper, lower = pl.ds(0, HALF * V), pl.ds(HALF * V, HALF * V)
    parts = {
        "tok1": (tok_hbm.at[lower], tok.at[lower]),
        "value": (value_hbm, w_value.at[:, pl.ds(0, D)]),
        "key": (key_hbm, w_key),
        "query": (query_hbm, query),
        "ocean": (ocean_hbm, ocean),
        "land": (land_hbm, land),
        "cot": (cot_hbm, cot),
        "tok0": (tok_hbm.at[upper], tok.at[upper]),
        "out": (out_hbm, w_out),
        "wo": (wo_hbm, w_o),
        "wq": (wq_hbm, w_q),
        "wk": (wk_hbm, w_k),
        "wv": (wv_hbm, w_v),
        "gain": (gain_hbm, gain),
        "plan": (plan_hbm, plan),
    }
    loads = {name: load(*ends, k) for k, (name, ends) in enumerate(parts.items())}

    early = ("cot", "tok1", "value", "key", "query", "ocean", "land")
    for name in early:
        loads[name].start()

    barrier = pltpu.get_barrier_semaphore()
    for to in (to_n, to_s, to_w, to_e, to_nw, to_se):
        pl.semaphore_signal(barrier, inc=1, device_id=to, device_id_type=MESH)

    def send(src, dst, to, slot):
        return pltpu.make_async_remote_copy(
            src_ref=src, dst_ref=dst, send_sem=send_sem.at[slot], recv_sem=recv_sem.at[slot],
            device_id=to, device_id_type=MESH,
        )

    def outward(home, region, slot):
        return [
            send(home.at[pl.ds(HALF, SIDE)], region.at[pl.ds(EDGE, SIDE)], to_s, slot),
            send(home.at[pl.ds(HALF + SIDE, EDGE)], region.at[pl.ds(0, EDGE)], to_se, slot + 1),
            send(home.at[pl.ds(SIDE, EDGE)], region.at[pl.ds(HALF, EDGE)], to_e, slot + 2),
        ]

    def inward(region, home, slot):
        return [
            send(region.at[pl.ds(EDGE, SIDE)], home.at[pl.ds(HALF, SIDE)], to_n, slot),
            send(region.at[pl.ds(0, EDGE)], home.at[pl.ds(HALF + SIDE, EDGE)], to_nw, slot + 1),
            send(region.at[pl.ds(HALF, EDGE)], home.at[pl.ds(SIDE, EDGE)], to_w, slot + 2),
        ]

    send_cot = outward(h_cot, r_cot, 0)
    send_cell = outward(h_cell, r_cell, 3)
    send_lay = inward(r_lay, h_lay, 6)
    send_grad = inward(r_grad, h_grad, 9)
    send_move = [
        send(move_out.at[0], move_in.at[0], to_e, 12),
        send(move_out.at[1], move_in.at[1], to_w, 13),
        send(move_out_p.at[0], move_in_p.at[0], to_e, 14),
        send(move_out_p.at[1], move_in_p.at[1], to_w, 15),
    ]

    loads["cot"].wait()
    quads = to_quads()
    for half in (1, 0):
        rows = pl.ds(half * HALF, HALF)
        h_cot[rows, :] = nn(quads, cot[rows, :]).astype(BF16)
    r_cot[pl.ds(HALF + EDGE, SIDE), :] = h_cot[pl.ds(0, SIDE), :]

    loads["tok1"].wait()
    loads["value"].wait()
    for name in loads:
        if name not in early:
            loads[name].start()

    def project_values(half, blocks=range(D // WIDE)):
        t_rows = slice(half * HALF * V, (half + 1) * HALF * V)
        for n in blocks:
            cols = slice(n * WIDE, (n + 1) * WIDE)
            values[t_rows, cols] = nn(tok[t_rows, :], w_value[:, cols]).astype(BF16)

    project_values(1, range(1))
    pl.semaphore_wait(barrier, 6)
    for copy in send_cot:
        copy.start()
    project_values(1, range(1, D // WIDE))

    loads["key"].wait()
    loads["query"].wait()
    picked = head_rows() * query[...][None, :]
    key_query = nt(picked, w_key[...]) * (1.0 / HD**0.5)
    high = key_query.astype(BF16)
    low = key_query - high.astype(F32)
    kq[...] = jnp.concatenate([high.astype(F32), low], axis=0).astype(BF16)

    loads["ocean"].wait()
    loads["land"].wait()
    rows16 = [ocean[r] for r in range(PLAT)] + [land[r] for r in range(PLAT)]
    there = jnp.concatenate(rows16, axis=0).astype(F32)
    shape = (PLON, N * V)
    there = nn(there, one_hot((iota(shape, 1) // V) % PLON == iota(shape, 0), F32))
    shape = there.shape
    line, spot = iota(shape, 0), iota(shape, 1)
    mine = ((line // 2) % PLAT == spot // ROW) & (4 + 2 * (line // 16) + line % 2 == spot % V)
    there = nn(jnp.ones((HEADS, 32), F32), jnp.where(mine, there, 0.0))
    live[...] = jnp.where(iota((HEADS, N * V), 1) % V < 4, 1.0, there)

    shape = (GROUP, SPAN)
    same_patch = iota(shape, 0) == iota(shape, 1) // V
    lane_head = iota(shape, 1) // HD
    heads_here = WIDE // HD

    for half in (1, 0):
        t_rows = slice(half * HALF * V, (half + 1) * HALF * V)
        if not half:
            loads["tok0"].wait()
            project_values(0)
        both = nt(kq[...], tok[t_rows, :])
        scores = stack(both[:HEADS] + both[HEADS:])
        scores = jnp.where(stack(live[:, t_rows]) > 0.5, scores, -1e30)
        expo = jnp.exp(scores - over_tokens(scores, jnp.maximum))
        prob = unstack(expo / over_tokens(expo, jnp.add))
        probs[:, t_rows] = prob
        for n in range(D // WIDE):
            cols = slice(n * WIDE, (n + 1) * WIDE)
            vals = values[t_rows, cols]
            for g in range(HALF // GROUP):
                span = slice(g * SPAN, (g + 1) * SPAN)
                weigh = [
                    jnp.where(same_patch, prob[h : h + 1, span], 0.0)
                    for h in range(n * heads_here, (n + 1) * heads_here)
                ]
                out = nn(jnp.concatenate(weigh, axis=0).astype(BF16), vals[span])
                pick = out[:GROUP]
                for h in range(1, heads_here):
                    pick = jnp.where(lane_head == h, out[h * GROUP : (h + 1) * GROUP], pick)
                first = half * HALF + g * GROUP
                mixed[first : first + GROUP, cols] = pick.astype(BF16)

        rows = pl.ds(half * HALF, HALF)
        if half:
            loads["out"].wait()
        cells = nn(mixed[rows, :], w_out[...]).astype(BF16)
        h_cell[rows, :] = nn(quads, cells).astype(BF16)
        if half:
            send_cell[0].start()
            send_cell[1].start()
    send_cell[2].start()
    r_cell[pl.ds(HALF + EDGE, SIDE), :] = h_cell[pl.ds(0, SIDE), :]

    for copy in send_cot:
        copy.wait_recv()
    loads["wo"].wait()
    b_mixdot[...] = nt(r_cot[...], w_o[...]).astype(BF16)

    deep = jnp.concatenate([kq[...].astype(F32), jnp.zeros((LANES - 2 * HEADS, D), F32)], axis=0)
    w_value[:, D:DEEP] = deep.T.astype(BF16)

    for copy in send_cell:
        copy.wait_recv()
    loads["gain"].wait()
    wide = r_cell[...].astype(F32)
    scale = lax.rsqrt(jnp.mean(wide * wide, axis=-1, keepdims=True) + EPS)
    normed[...] = (wide * scale * gain[...].astype(F32)[None, :]).astype(BF16)
    for name, weight, out in (("wq", w_q, b_q), ("wk", w_k, b_k), ("wv", w_v, b_v)):
        loads[name].wait()
        out[...] = nn(normed[...], weight[...]).astype(BF16)

    patches = WIN * WIN
    half_win = patches // 2
    pole = i == 0
    own_head = one_hot(iota((WIDE, WIDE), 0) // patches == iota((WIDE, WIDE), 1) // HD)
    far = (iota((patches, WIDE), 0) < half_win) != (iota((patches, WIDE), 1) % patches < half_win)
    bias = jnp.where(far & pole, -1e30, 0.0)
    win_head = iota((patches, WIDE), 1) // HD

    def per_head(x):
        return jnp.concatenate([x] * (WIDE // HD), axis=0) * own_head

    def own_blocks(x):
        out = x[0:patches]
        for h in range(1, WIDE // HD):
            out = jnp.where(win_head == h, x[h * patches : (h + 1) * patches], out)
        return out

    wins = range(N // patches)
    for g in range(D // WIDE):
        cols = slice(g * WIDE, (g + 1) * WIDE)

        def get(ref, w):
            upper = ref[w * half_win : (w + 1) * half_win, cols]
            lower = ref[HALF + w * half_win : HALF + (w + 1) * half_win, cols]
            return jnp.concatenate([upper, lower], axis=0)

        def put(ref, w, x):
            x = x.astype(BF16)
            ref[w * half_win : (w + 1) * half_win, cols] = x[:half_win]
            ref[HALF + w * half_win : HALF + (w + 1) * half_win, cols] = x[half_win:]

        keys, vals = [get(b_k, w) for w in wins], [get(b_v, w) for w in wins]
        queries = [per_head(get(b_q, w)) for w in wins]
        scores = [nt(keys[w], queries[w]) * (1.0 / HD**0.5) + bias for w in wins]
        mixdot = [per_head(get(b_mixdot, w)) for w in wins]
        d_prob = [nt(vals[w], mixdot[w]) for w in wins]
        expo = [jnp.exp(scores[w] - jnp.max(scores[w], axis=0, keepdims=True)) for w in wins]
        prob = [expo[w] / jnp.sum(expo[w], axis=0, keepdims=True) for w in wins]
        prob_b = [prob[w].astype(BF16) for w in wins]
        for w in wins:
            put(d_v, w, nn(prob_b[w], mixdot[w]))
        inner = [jnp.sum(d_prob[w] * prob[w], axis=0, keepdims=True) for w in wins]
        d_score = [
            (prob[w] * (d_prob[w] - inner[w]) * (1.0 / HD**0.5)).astype(BF16) for w in wins
        ]
        for w in wins:
            put(b_mix, w, own_blocks(tn(prob_b[w], vals[w])))
        for w in wins:
            put(d_k, w, nn(d_score[w], queries[w]))
        for w in wins:
            put(d_q, w, own_blocks(tn(d_score[w], keys[w])))

    d_norm = nt(d_q[...], w_q[...]) + nt(d_k[...], w_k[...]) + nt(d_v[...], w_v[...])
    wide = r_cell[...].astype(F32)
    scale = lax.rsqrt(jnp.mean(wide * wide, axis=-1, keepdims=True) + EPS)
    d_unit = d_norm * gain[...].astype(F32)[None, :]
    along = jnp.mean(wide * d_unit, axis=-1, keepdims=True)
    grad = r_cot[...].astype(F32) + scale * d_unit - wide * (scale * scale * scale * along)
    r_grad[...] = grad.astype(BF16)
    for copy in send_grad:
        copy.start()
    h_grad[pl.ds(0, SIDE), :] = r_grad[pl.ds(HALF + EDGE, SIDE), :]

    result = r_cell[...].astype(F32) + nn(b_mix[...], w_o[...])
    r_lay[...] = result.astype(BF16)
    h_lay[pl.ds(0, SIDE), :] = r_lay[pl.ds(HALF + EDGE, SIDE), :]
    rows_of = from_quads()
    shape = (heads_here * GROUP, WIDE)
    own_lanes = one_hot(iota(shape, 0) // GROUP == iota(shape, 1) // HD)
    two = 2 * PLON
    expand = one_hot(iota((two * V, two), 0) // V == iota((two * V, two), 1))
    heads = head_rows()
    loads["plan"].wait()
    index = (plan[0, 0], plan[0, 1])

    def agg_back(half):
        rows, t_rows = pl.ds(half * HALF, HALF), slice(half * HALF * V, (half + 1) * HALF * V)
        cell_grad = nn(rows_of, h_grad[rows, :]).astype(BF16)
        d_mixed[rows, :] = nt(cell_grad, w_out[...]).astype(BF16)
        for g in range(half * HALF // GROUP, (half + 1) * HALF // GROUP):
            group, span = slice(g * GROUP, (g + 1) * GROUP), slice(g * SPAN, (g + 1) * SPAN)
            for n in range(D // WIDE):
                cols = slice(n * WIDE, (n + 1) * WIDE)
                spread = jnp.concatenate([d_mixed[group, cols]] * heads_here, axis=0) * own_lanes
                out = nt(spread, values[span, cols])
                for h in range(heads_here):
                    part = jnp.where(same_patch, out[h * GROUP : (h + 1) * GROUP], 0.0)
                    head = n * heads_here + h
                    d_probs[head : head + 1, span] = jnp.sum(part, axis=0, keepdims=True)
        prob, d_prob = stack(probs[:, t_rows]), stack(d_probs[:, t_rows])
        d_probs[:, t_rows] = unstack(prob * (d_prob - over_tokens(prob * d_prob, jnp.add)))

    def token_back(first, prob, d_score, here):
        t_rows = pl.ds(first * V, two * V)
        for n in range(D // WIDE):
            cols = slice(n * WIDE, (n + 1) * WIDE)
            wide = tn(prob, heads[:, cols]) * nn(expand, here[:, cols])
            d_values[t_rows, cols] = wide.astype(BF16)
        pad = jnp.zeros((LANES - 2 * HEADS, two * V), F32)
        d_values[t_rows, D:DEEP] = jnp.concatenate([d_score, d_score, pad], axis=0).T.astype(BF16)

    def multiply(first, count):
        t_rows = pl.ds(first * V, count * V)
        for n in range(D // WIDE):
            cols = slice(n * WIDE, (n + 1) * WIDE)
            grad_out[t_rows, cols] = nt(d_values[t_rows, :], w_value[cols, :]).astype(BF16)

    def half_back(half):
        for c in range(2 * half, 2 * half + 2):
            t_rows = slice(c * two * V, (c + 1) * two * V)
            row = 2 * c + iota((two, D), 0) // PLON
            kept = (row != index[0]) & (row != index[1])
            here = d_mixed[c * two : (c + 1) * two, :].astype(F32)
            here = jnp.where(kept, here, 0.0).astype(BF16)
            row = 2 * c + iota((HEADS, two * V), 1) // ROW
            kept = (row != index[0]) & (row != index[1])
            d_score = jnp.where(kept, d_probs[:, t_rows], 0.0)
            token_back(c * two, probs[:, t_rows].astype(BF16), d_score, here)
        multiply(half * HALF, HALF)

    send_grad[2].wait_recv()
    agg_back(0)
    for copy in send_lay:
        copy.start()
    half_back(0)
    send_grad[0].wait_recv()
    send_grad[1].wait_recv()
    agg_back(1)

    shape = (PLON, N)
    for k, name in enumerate(index):
        start = jnp.where(name >= 0, name * PLON, -N)
        picked = nn(one_hot(start + iota(shape, 0) == iota(shape, 1)), d_mixed[...])
        pad = jnp.zeros((32 - PLON, D), F32)
        move_out[k] = jnp.concatenate([picked, pad], axis=0).astype(BF16)
        row = jnp.zeros((2 * HEADS, ROW), F32)
        for r in range(PLAT):
            lanes = slice(r * ROW, (r + 1) * ROW)
            here = jnp.concatenate([probs[:, lanes], d_probs[:, lanes]], axis=0)
            row = jnp.where(name == r, here, row)
        pad = jnp.zeros((2 * HEADS, WIDE - ROW), F32)
        move_out_p[k] = jnp.concatenate([row, pad], axis=1).astype(BF16)
        send_move[k].start()
        send_move[2 + k].start()

    half_back(1)
    for copy in send_move:
        copy.wait_recv()
    arrived = [move_in[k].astype(F32)[:PLON] for k in range(2)]
    here = jnp.concatenate(arrived, axis=0).astype(BF16)
    arrived = [move_in_p[k].astype(F32)[:, :ROW] for k in range(2)]
    arrived = jnp.concatenate(arrived, axis=1)
    token_back(N, arrived[:HEADS].astype(BF16), arrived[HEADS:], here)
    multiply(N, two)
    for copy in send_lay:
        copy.wait_recv()
    for half in (0, 1):
        rows = slice(half * HALF, (half + 1) * HALF)
        lay_ref[rows, :] = nn(rows_of, h_lay[rows, :]).astype(BF16)
    for copy in send_cot + send_cell + send_lay + send_grad + send_move:
        copy.wait_send()


def body(
    n_lat, n_lon,
    var_tokens, ocean_mask, land_mask, move_plan, agg_query, agg_key, agg_value, agg_out,
    norm_gain, win_query, win_key, win_value, win_out, out_cotangent,
):
    hbm = pl.BlockSpec(memory_space=pltpu.HBM)
    vmem = pl.BlockSpec(memory_space=pltpu.VMEM)
    weight = pltpu.VMEM((D, D), BF16)
    patch = pltpu.VMEM((N, D), BF16)
    layer_out, token_grad = pl.pallas_call(
        functools.partial(layer, n_lat, n_lon),
        out_shape=(pltpu.VMEM((N, D), BF16), pltpu.VMEM((TOKENS, D), BF16)),
        in_specs=[hbm] * 14,
        out_specs=(vmem, vmem),
        scratch_shapes=[pltpu.VMEM((N * V, D), BF16)]
        + [weight, pltpu.VMEM((D, DEEP), BF16)]
        + [weight] * 5
        + [patch]
        + [pltpu.VMEM((PLAT, 2, PLON), jnp.int32)] * 2
        + [pltpu.VMEM((D,), BF16)] * 2
        + [pltpu.SMEM((1, 2), jnp.int32)]
        + [pltpu.VMEM((N * V, D), BF16), pltpu.VMEM((TOKENS, DEEP), BF16)]
        + [pltpu.VMEM((HEADS, N * V), F32)] * 2
        + [patch] * 2
        + [pltpu.VMEM((HEADS, N * V), F32), pltpu.VMEM((2 * HEADS, D), BF16)]
        + [patch] * 8
        + [patch] * 9
        + [pltpu.VMEM((2, 32, D), BF16)] * 2
        + [pltpu.VMEM((2, 2 * HEADS, WIDE), BF16)] * 2
        + [
            pltpu.SemaphoreType.DMA((15,)),
            pltpu.SemaphoreType.DMA((16,)),
            pltpu.SemaphoreType.DMA((16,)),
        ],
        compiler_params=pltpu.CompilerParams(
            collective_id=0, has_side_effects=True, vmem_limit_bytes=56 * 1024 * 1024
        ),
        name="layer",
    )(
        var_tokens.reshape(N * V, D),
        jnp.transpose(ocean_mask, (0, 2, 1)),
        jnp.transpose(land_mask, (0, 2, 1)),
        move_plan.reshape(1, 2),
        agg_query,
        norm_gain,
        agg_key, agg_value, agg_out, win_query, win_key, win_value, win_out,
        out_cotangent.reshape(N, D),
    )

    return (
        layer_out.reshape(PLAT, PLON, D),
        token_grad.reshape(PLAT + 2, PLON, V, D),
    )


def solution(mesh):
    placed = P("lat", "lon", None)
    return jax.shard_map(
        functools.partial(body, mesh.shape["lat"], mesh.shape["lon"]),
        mesh=mesh,
        in_specs=(P("lat", "lon", None, None), placed, placed, placed) + (P(),) * 9 + (placed,),
        out_specs=(placed, P("lat", "lon", None, None)),
        check_vma=False,
    )
```

```python
import functools

import jax
import jax.numpy as jnp
from jax import lax
from jax.experimental import pallas as pl
from jax.experimental.pallas import tpu as pltpu
from jax.sharding import PartitionSpec as P

MESH = pl.DeviceIdType.MESH
HEADS = 16
WIN = 8
EPS = 1e-06
F32 = jnp.float32
BF16 = jnp.bfloat16

D = 1024
HD = D // HEADS
V = 8
PLAT = 8
PLON = 24
N = PLAT * PLON
ROW = PLON * V
LANES = 128
WIDE = 256
HALF = N // 2
EDGE = 16
SIDE = 80
GROUP = 32
SPAN = GROUP * V
DEEP = D + LANES
TOKENS = (PLAT + 2) * ROW


def iota(shape, dim):
    return lax.broadcasted_iota(jnp.int32, shape, dim)


def one_hot(mask, dtype=BF16):
    return jnp.where(mask, 1.0, 0.0).astype(dtype)


def nn(a, b):
    return lax.dot_general(a, b, (((1,), (0,)), ((), ())), preferred_element_type=F32)


def nt(a, b):
    return lax.dot_general(a, b, (((1,), (1,)), ((), ())), preferred_element_type=F32)


def tn(a, b):
    return lax.dot_general(a, b, (((0,), (0,)), ((), ())), preferred_element_type=F32)


def head_rows():
    return one_hot(iota((HEADS, D), 0) == iota((HEADS, D), 1) // HD)


def stack(x):
    return jnp.concatenate([x[:, k : k + LANES] for k in range(0, x.shape[1], LANES)], axis=0)


def unstack(x):
    return jnp.concatenate([x[k : k + HEADS] for k in range(0, x.shape[0], HEADS)], axis=1)


def over_tokens(x, op):
    lane = iota(x.shape, 1)
    for step in (1, 2, 4):
        other = jnp.where(
            lane & step == 0, pltpu.roll(x, LANES - step, axis=1), pltpu.roll(x, step, axis=1)
        )
        x = op(x, other)
    return x


def to_quads():
    n, m = iota((HALF, HALF), 0), iota((HALF, HALF), 1)
    return one_hot(((n % 16) // 4) * PLON + (n // 16) * 4 + n % 4 == m)


def from_quads():
    n, m = iota((HALF, HALF), 1), iota((HALF, HALF), 0)
    return one_hot(((n % 16) // 4) * PLON + (n // 16) * 4 + n % 4 == m)


def layer(
    n_lat, n_lon,
    tok_hbm, ocean_hbm, land_hbm, plan_hbm, query_hbm, gain_hbm,
    key_hbm, value_hbm, out_hbm, wq_hbm, wk_hbm, wv_hbm, wo_hbm, cot_hbm,
    lay_ref, grad_out,
    tok, w_key, w_value, w_out, w_q, w_k, w_v, w_o, cot,
    ocean, land, query, gain, plan,
    values, d_values, probs, d_probs, mixed, d_mixed, live, kq,
    h_cot, h_cell, h_lay, h_grad, r_cot, r_cell, r_lay, r_grad,
    normed, b_q, b_k, b_v, b_mixdot, b_mix, d_q, d_k, d_v,
    move_out, move_in, move_out_p, move_in_p,
    load_sem, send_sem, recv_sem,
):
    i, j = lax.axis_index("lat"), lax.axis_index("lon")
    north, south = lax.rem(i + n_lat - 1, n_lat), lax.rem(i + 1, n_lat)
    west, east = lax.rem(j + n_lon - 1, n_lon), lax.rem(j + 1, n_lon)
    to_n, to_s, to_w, to_e = (north, j), (south, j), (i, west), (i, east)
    to_nw, to_se = (north, west), (south, east)

    def load(src, dst, slot):
        return pltpu.make_async_copy(src, dst, load_sem.at[slot])

    upper, lower = pl.ds(0, HALF * V), pl.ds(HALF * V, HALF * V)
    parts = {
        "tok1": (tok_hbm.at[lower], tok.at[lower]),
        "value": (value_hbm, w_value.at[:, pl.ds(0, D)]),
        "key": (key_hbm, w_key),
        "query": (query_hbm, query),
        "ocean": (ocean_hbm, ocean),
        "land": (land_hbm, land),
        "cot": (cot_hbm, cot),
        "tok0": (tok_hbm.at[upper], tok.at[upper]),
        "out": (out_hbm, w_out),
        "wo": (wo_hbm, w_o),
        "wq": (wq_hbm, w_q),
        "wk": (wk_hbm, w_k),
        "wv": (wv_hbm, w_v),
        "gain": (gain_hbm, gain),
        "plan": (plan_hbm, plan),
    }
    loads = {name: load(*ends, k) for k, (name, ends) in enumerate(parts.items())}

    early = ("cot", "tok1", "value", "key", "query", "ocean", "land")
    for name in early:
        loads[name].start()

    barrier = pltpu.get_barrier_semaphore()
    for to in (to_n, to_s, to_w, to_e, to_nw, to_se):
        pl.semaphore_signal(barrier, inc=1, device_id=to, device_id_type=MESH)

    def send(src, dst, to, slot):
        return pltpu.make_async_remote_copy(
            src_ref=src, dst_ref=dst, send_sem=send_sem.at[slot], recv_sem=recv_sem.at[slot],
            device_id=to, device_id_type=MESH,
        )

    def outward(home, region, slot):
        return [
            send(home.at[pl.ds(HALF, SIDE)], region.at[pl.ds(EDGE, SIDE)], to_s, slot),
            send(home.at[pl.ds(HALF + SIDE, EDGE)], region.at[pl.ds(0, EDGE)], to_se, slot + 1),
            send(home.at[pl.ds(SIDE, EDGE)], region.at[pl.ds(HALF, EDGE)], to_e, slot + 2),
        ]

    def inward(region, home, slot):
        return [
            send(region.at[pl.ds(EDGE, SIDE)], home.at[pl.ds(HALF, SIDE)], to_n, slot),
            send(region.at[pl.ds(0, EDGE)], home.at[pl.ds(HALF + SIDE, EDGE)], to_nw, slot + 1),
            send(region.at[pl.ds(HALF, EDGE)], home.at[pl.ds(SIDE, EDGE)], to_w, slot + 2),
        ]

    send_cot = outward(h_cot, r_cot, 0)
    send_cell = outward(h_cell, r_cell, 3)
    send_lay = inward(r_lay, h_lay, 6)
    send_grad = inward(r_grad, h_grad, 9)
    send_move = [
        send(move_out.at[0], move_in.at[0], to_e, 12),
        send(move_out.at[1], move_in.at[1], to_w, 13),
        send(move_out_p.at[0], move_in_p.at[0], to_e, 14),
        send(move_out_p.at[1], move_in_p.at[1], to_w, 15),
    ]

    loads["cot"].wait()
    quads = to_quads()
    for half in (1, 0):
        rows = pl.ds(half * HALF, HALF)
        h_cot[rows, :] = nn(quads, cot[rows, :]).astype(BF16)
    r_cot[pl.ds(HALF + EDGE, SIDE), :] = h_cot[pl.ds(0, SIDE), :]

    loads["tok1"].wait()
    loads["value"].wait()
    for name in loads:
        if name not in early:
            loads[name].start()

    def project_values(half, blocks=range(D // WIDE)):
        t_rows = slice(half * HALF * V, (half + 1) * HALF * V)
        for n in blocks:
            cols = slice(n * WIDE, (n + 1) * WIDE)
            values[t_rows, cols] = nn(tok[t_rows, :], w_value[:, cols]).astype(BF16)

    project_values(1, range(1))
    pl.semaphore_wait(barrier, 6)
    for copy in send_cot:
        copy.start()
    project_values(1, range(1, D // WIDE))

    loads["key"].wait()
    loads["query"].wait()
    picked = head_rows() * query[...][None, :]
    key_query = nt(picked, w_key[...]) * (1.0 / HD**0.5)
    high = key_query.astype(BF16)
    low = key_query - high.astype(F32)
    kq[...] = jnp.concatenate([high.astype(F32), low], axis=0).astype(BF16)

    loads["ocean"].wait()
    loads["land"].wait()
    rows16 = [ocean[r] for r in range(PLAT)] + [land[r] for r in range(PLAT)]
    there = jnp.concatenate(rows16, axis=0).astype(F32)
    shape = (PLON, N * V)
    there = nn(there, one_hot((iota(shape, 1) // V) % PLON == iota(shape, 0), F32))
    shape = there.shape
    line, spot = iota(shape, 0), iota(shape, 1)
    mine = ((line // 2) % PLAT == spot // ROW) & (4 + 2 * (line // 16) + line % 2 == spot % V)
    there = nn(jnp.ones((HEADS, 32), F32), jnp.where(mine, there, 0.0))
    live[...] = jnp.where(iota((HEADS, N * V), 1) % V < 4, 1.0, there)

    shape = (GROUP, SPAN)
    same_patch = iota(shape, 0) == iota(shape, 1) // V
    lane_head = iota(shape, 1) // HD
    heads_here = WIDE // HD

    for half in (1, 0):
        t_rows = slice(half * HALF * V, (half + 1) * HALF * V)
        if not half:
            loads["tok0"].wait()
            project_values(0)
        both = nt(kq[...], tok[t_rows, :])
        scores = stack(both[:HEADS] + both[HEADS:])
        scores = jnp.where(stack(live[:, t_rows]) > 0.5, scores, -1e30)
        expo = jnp.exp(scores - over_tokens(scores, jnp.maximum))
        prob = unstack(expo / over_tokens(expo, jnp.add))
        probs[:, t_rows] = prob
        for n in range(D // WIDE):
            cols = slice(n * WIDE, (n + 1) * WIDE)
            vals = values[t_rows, cols]
            for g in range(HALF // GROUP):
                span = slice(g * SPAN, (g + 1) * SPAN)
                weigh = [
                    jnp.where(same_patch, prob[h : h + 1, span], 0.0)
                    for h in range(n * heads_here, (n + 1) * heads_here)
                ]
                out = nn(jnp.concatenate(weigh, axis=0).astype(BF16), vals[span])
                pick = out[:GROUP]
                for h in range(1, heads_here):
                    pick = jnp.where(lane_head == h, out[h * GROUP : (h + 1) * GROUP], pick)
                first = half * HALF + g * GROUP
                mixed[first : first + GROUP, cols] = pick.astype(BF16)

        rows = pl.ds(half * HALF, HALF)
        if half:
            loads["out"].wait()
        cells = nn(mixed[rows, :], w_out[...]).astype(BF16)
        h_cell[rows, :] = nn(quads, cells).astype(BF16)
        if half:
            send_cell[0].start()
            send_cell[1].start()
    send_cell[2].start()
    r_cell[pl.ds(HALF + EDGE, SIDE), :] = h_cell[pl.ds(0, SIDE), :]

    for copy in send_cot:
        copy.wait_recv()
    loads["wo"].wait()
    b_mixdot[...] = nt(r_cot[...], w_o[...]).astype(BF16)

    deep = jnp.concatenate([kq[...].astype(F32), jnp.zeros((LANES - 2 * HEADS, D), F32)], axis=0)
    w_value[:, D:DEEP] = deep.T.astype(BF16)

    for copy in send_cell:
        copy.wait_recv()
    loads["gain"].wait()
    wide = r_cell[...].astype(F32)
    scale = lax.rsqrt(jnp.mean(wide * wide, axis=-1, keepdims=True) + EPS)
    normed[...] = (wide * scale * gain[...].astype(F32)[None, :]).astype(BF16)
    for name, weight, out in (("wq", w_q, b_q), ("wk", w_k, b_k), ("wv", w_v, b_v)):
        loads[name].wait()
        out[...] = nn(normed[...], weight[...]).astype(BF16)

    patches = WIN * WIN
    half_win = patches // 2
    pole = i == 0
    own_head = one_hot(iota((WIDE, WIDE), 0) // patches == iota((WIDE, WIDE), 1) // HD)
    far = (iota((patches, WIDE), 0) < half_win) != (iota((patches, WIDE), 1) % patches < half_win)
    bias = jnp.where(far & pole, -1e30, 0.0)
    win_head = iota((patches, WIDE), 1) // HD

    def per_head(x):
        return jnp.concatenate([x] * (WIDE // HD), axis=0) * own_head

    def own_blocks(x):
        out = x[0:patches]
        for h in range(1, WIDE // HD):
            out = jnp.where(win_head == h, x[h * patches : (h + 1) * patches], out)
        return out

    wins = range(N // patches)
    for g in range(D // WIDE):
        cols = slice(g * WIDE, (g + 1) * WIDE)

        def get(ref, w):
            upper = ref[w * half_win : (w + 1) * half_win, cols]
            lower = ref[HALF + w * half_win : HALF + (w + 1) * half_win, cols]
            return jnp.concatenate([upper, lower], axis=0)

        def put(ref, w, x):
            x = x.astype(BF16)
            ref[w * half_win : (w + 1) * half_win, cols] = x[:half_win]
            ref[HALF + w * half_win : HALF + (w + 1) * half_win, cols] = x[half_win:]

        keys, vals = [get(b_k, w) for w in wins], [get(b_v, w) for w in wins]
        queries = [per_head(get(b_q, w)) for w in wins]
        scores = [nt(keys[w], queries[w]) * (1.0 / HD**0.5) + bias for w in wins]
        mixdot = [per_head(get(b_mixdot, w)) for w in wins]
        d_prob = [nt(vals[w], mixdot[w]) for w in wins]
        expo = [jnp.exp(scores[w] - jnp.max(scores[w], axis=0, keepdims=True)) for w in wins]
        prob = [expo[w] / jnp.sum(expo[w], axis=0, keepdims=True) for w in wins]
        prob_b = [prob[w].astype(BF16) for w in wins]
        for w in wins:
            put(d_v, w, nn(prob_b[w], mixdot[w]))
        inner = [jnp.sum(d_prob[w] * prob[w], axis=0, keepdims=True) for w in wins]
        d_score = [
            (prob[w] * (d_prob[w] - inner[w]) * (1.0 / HD**0.5)).astype(BF16) for w in wins
        ]
        for w in wins:
            put(b_mix, w, own_blocks(tn(prob_b[w], vals[w])))
        for w in wins:
            put(d_k, w, nn(d_score[w], queries[w]))
        for w in wins:
            put(d_q, w, own_blocks(tn(d_score[w], keys[w])))

    d_norm = nt(d_q[...], w_q[...]) + nt(d_k[...], w_k[...]) + nt(d_v[...], w_v[...])
    wide = r_cell[...].astype(F32)
    scale = lax.rsqrt(jnp.mean(wide * wide, axis=-1, keepdims=True) + EPS)
    d_unit = d_norm * gain[...].astype(F32)[None, :]
    along = jnp.mean(wide * d_unit, axis=-1, keepdims=True)
    grad = r_cot[...].astype(F32) + scale * d_unit - wide * (scale * scale * scale * along)
    r_grad[...] = grad.astype(BF16)
    for copy in send_grad:
        copy.start()
    h_grad[pl.ds(0, SIDE), :] = r_grad[pl.ds(HALF + EDGE, SIDE), :]

    result = r_cell[...].astype(F32) + nn(b_mix[...], w_o[...])
    r_lay[...] = result.astype(BF16)
    h_lay[pl.ds(0, SIDE), :] = r_lay[pl.ds(HALF + EDGE, SIDE), :]
    rows_of = from_quads()
    shape = (heads_here * GROUP, WIDE)
    own_lanes = one_hot(iota(shape, 0) // GROUP == iota(shape, 1) // HD)
    two = 2 * PLON
    expand = one_hot(iota((two * V, two), 0) // V == iota((two * V, two), 1))
    heads = head_rows()
    loads["plan"].wait()
    index = (plan[0, 0], plan[0, 1])

    def agg_back(half):
        rows, t_rows = pl.ds(half * HALF, HALF), slice(half * HALF * V, (half + 1) * HALF * V)
        cell_grad = nn(rows_of, h_grad[rows, :]).astype(BF16)
        d_mixed[rows, :] = nt(cell_grad, w_out[...]).astype(BF16)
        for g in range(half * HALF // GROUP, (half + 1) * HALF // GROUP):
            group, span = slice(g * GROUP, (g + 1) * GROUP), slice(g * SPAN, (g + 1) * SPAN)
            for n in range(D // WIDE):
                cols = slice(n * WIDE, (n + 1) * WIDE)
                spread = jnp.concatenate([d_mixed[group, cols]] * heads_here, axis=0) * own_lanes
                out = nt(spread, values[span, cols])
                for h in range(heads_here):
                    part = jnp.where(same_patch, out[h * GROUP : (h + 1) * GROUP], 0.0)
                    head = n * heads_here + h
                    d_probs[head : head + 1, span] = jnp.sum(part, axis=0, keepdims=True)
        prob, d_prob = stack(probs[:, t_rows]), stack(d_probs[:, t_rows])
        d_probs[:, t_rows] = unstack(prob * (d_prob - over_tokens(prob * d_prob, jnp.add)))

    def token_back(first, prob, d_score, here):
        t_rows = pl.ds(first * V, two * V)
        for n in range(D // WIDE):
            cols = slice(n * WIDE, (n + 1) * WIDE)
            wide = tn(prob, heads[:, cols]) * nn(expand, here[:, cols])
            d_values[t_rows, cols] = wide.astype(BF16)
        pad = jnp.zeros((LANES - 2 * HEADS, two * V), F32)
        d_values[t_rows, D:DEEP] = jnp.concatenate([d_score, d_score, pad], axis=0).T.astype(BF16)

    def multiply(first, count):
        t_rows = pl.ds(first * V, count * V)
        for n in range(D // WIDE):
            cols = slice(n * WIDE, (n + 1) * WIDE)
            grad_out[t_rows, cols] = nt(d_values[t_rows, :], w_value[cols, :]).astype(BF16)

    def half_back(half):
        for c in range(2 * half, 2 * half + 2):
            t_rows = slice(c * two * V, (c + 1) * two * V)
            row = 2 * c + iota((two, D), 0) // PLON
            kept = (row != index[0]) & (row != index[1])
            here = d_mixed[c * two : (c + 1) * two, :].astype(F32)
            here = jnp.where(kept, here, 0.0).astype(BF16)
            row = 2 * c + iota((HEADS, two * V), 1) // ROW
            kept = (row != index[0]) & (row != index[1])
            d_score = jnp.where(kept, d_probs[:, t_rows], 0.0)
            token_back(c * two, probs[:, t_rows].astype(BF16), d_score, here)
        multiply(half * HALF, HALF)

    send_grad[2].wait_recv()
    agg_back(0)
    half_back(0)
    send_grad[0].wait_recv()
    send_grad[1].wait_recv()
    agg_back(1)

    shape = (PLON, N)
    for k, name in enumerate(index):
        start = jnp.where(name >= 0, name * PLON, -N)
        picked = nn(one_hot(start + iota(shape, 0) == iota(shape, 1)), d_mixed[...])
        pad = jnp.zeros((32 - PLON, D), F32)
        move_out[k] = jnp.concatenate([picked, pad], axis=0).astype(BF16)
        row = jnp.zeros((2 * HEADS, ROW), F32)
        for r in range(PLAT):
            lanes = slice(r * ROW, (r + 1) * ROW)
            here = jnp.concatenate([probs[:, lanes], d_probs[:, lanes]], axis=0)
            row = jnp.where(name == r, here, row)
        pad = jnp.zeros((2 * HEADS, WIDE - ROW), F32)
        move_out_p[k] = jnp.concatenate([row, pad], axis=1).astype(BF16)
        send_move[k].start()
        send_move[2 + k].start()
    for copy in send_lay:
        copy.start()

    half_back(1)
    for copy in send_move:
        copy.wait_recv()
    arrived = [move_in[k].astype(F32)[:PLON] for k in range(2)]
    here = jnp.concatenate(arrived, axis=0).astype(BF16)
    arrived = [move_in_p[k].astype(F32)[:, :ROW] for k in range(2)]
    arrived = jnp.concatenate(arrived, axis=1)
    token_back(N, arrived[:HEADS].astype(BF16), arrived[HEADS:], here)
    multiply(N, two)
    for copy in send_lay:
        copy.wait_recv()
    for half in (0, 1):
        rows = slice(half * HALF, (half + 1) * HALF)
        lay_ref[rows, :] = nn(rows_of, h_lay[rows, :]).astype(BF16)
    for copy in send_cot + send_cell + send_lay + send_grad + send_move:
        copy.wait_send()


def body(
    n_lat, n_lon,
    var_tokens, ocean_mask, land_mask, move_plan, agg_query, agg_key, agg_value, agg_out,
    norm_gain, win_query, win_key, win_value, win_out, out_cotangent,
):
    hbm = pl.BlockSpec(memory_space=pltpu.HBM)
    vmem = pl.BlockSpec(memory_space=pltpu.VMEM)
    weight = pltpu.VMEM((D, D), BF16)
    patch = pltpu.VMEM((N, D), BF16)
    layer_out, token_grad = pl.pallas_call(
        functools.partial(layer, n_lat, n_lon),
        out_shape=(pltpu.VMEM((N, D), BF16), pltpu.VMEM((TOKENS, D), BF16)),
        in_specs=[hbm] * 14,
        out_specs=(vmem, vmem),
        scratch_shapes=[pltpu.VMEM((N * V, D), BF16)]
        + [weight, pltpu.VMEM((D, DEEP), BF16)]
        + [weight] * 5
        + [patch]
        + [pltpu.VMEM((PLAT, 2, PLON), jnp.int32)] * 2
        + [pltpu.VMEM((D,), BF16)] * 2
        + [pltpu.SMEM((1, 2), jnp.int32)]
        + [pltpu.VMEM((N * V, D), BF16), pltpu.VMEM((TOKENS, DEEP), BF16)]
        + [pltpu.VMEM((HEADS, N * V), F32)] * 2
        + [patch] * 2
        + [pltpu.VMEM((HEADS, N * V), F32), pltpu.VMEM((2 * HEADS, D), BF16)]
        + [patch] * 8
        + [patch] * 9
        + [pltpu.VMEM((2, 32, D), BF16)] * 2
        + [pltpu.VMEM((2, 2 * HEADS, WIDE), BF16)] * 2
        + [
            pltpu.SemaphoreType.DMA((15,)),
            pltpu.SemaphoreType.DMA((16,)),
            pltpu.SemaphoreType.DMA((16,)),
        ],
        compiler_params=pltpu.CompilerParams(
            collective_id=0, has_side_effects=True, vmem_limit_bytes=56 * 1024 * 1024
        ),
        name="layer",
    )(
        var_tokens.reshape(N * V, D),
        jnp.transpose(ocean_mask, (0, 2, 1)),
        jnp.transpose(land_mask, (0, 2, 1)),
        move_plan.reshape(1, 2),
        agg_query,
        norm_gain,
        agg_key, agg_value, agg_out, win_query, win_key, win_value, win_out,
        out_cotangent.reshape(N, D),
    )

    return (
        layer_out.reshape(PLAT, PLON, D),
        token_grad.reshape(PLAT + 2, PLON, V, D),
    )


def solution(mesh):
    placed = P("lat", "lon", None)
    return jax.shard_map(
        functools.partial(body, mesh.shape["lat"], mesh.shape["lon"]),
        mesh=mesh,
        in_specs=(P("lat", "lon", None, None), placed, placed, placed) + (P(),) * 9 + (placed,),
        out_specs=(placed, P("lat", "lon", None, None)),
        check_vma=False,
    )
```
